32 devices in a mesh: rep: 4 (over z), shard: 8 (over y, x, core).
Axes of the slice: x: 2, y: 2, z: 4, core: 2. Of those that a mesh axis runs over, the one named last changes fastest.
Arguments:
- hidden: bfloat16 [32768, 1024], P(('rep', 'shard')), may hold values from -6 to 6
- segments: int32 [32768], P(('rep', 'shard')), may hold values from 0 to 63, never falling along the last dimension, each value on 1 to 1024 neighbouring positions
- pad_mask: int32 [32768], P(('rep', 'shard')), may hold values from 0 to 1, as said below
- encoder: bfloat16 [32, 1024, 1024], P(('rep', 'shard')), may hold values from -6 to 6
- src_len: int32 [32], P(('rep', 'shard')), may hold values from 256 to 1024
- grad_out: bfloat16 [32768, 1024], P(('rep', 'shard')), may hold values from -6 to 6
- ln_gain: bfloat16 [3, 1024], P(None, 'shard'), may hold values from 0.099609375 to 1.8984375
- self_qkv: bfloat16 [1024, 3072], P('shard'), may hold values from -0.1875 to 0.1875
- self_out: bfloat16 [1024, 1024], P('shard'), may hold values from -0.375 to 0.375
- self_vec: bfloat16 [4096], P('shard'), may hold values from -3 to 3
- cross_qkv: bfloat16 [1024, 3072], P('shard'), may hold values from -0.1875 to 0.1875
- cross_out: bfloat16 [1024, 1024], P('shard'), may hold values from -0.375 to 0.375
- cross_vec: bfloat16 [4096], P('shard'), may hold values from -3 to 3
- fc_in: bfloat16 [1024, 8192], P('shard'), may hold values from -0.1875 to 0.1875
- fc_out: bfloat16 [8192, 1024], P('shard'), may hold values from -0.09375 to 0.09375
- mlp_vec: bfloat16 [10240], P('shard'), may hold values from -3 to 3
Outputs:
- output: bfloat16 [32768, 1024], P(('rep', 'shard'))
- grad_hidden: bfloat16 [32768, 1024], P(('rep', 'shard'))
- grad_encoder: bfloat16 [32, 1024, 1024], P(('rep', 'shard'))
- grad_ln_gain: float32 [3, 1024], P(None, 'shard')
- grad_self_qkv: float32 [1024, 3072], P('shard')
- grad_self_out: float32 [1024, 1024], P('shard')
- grad_self_vec: float32 [4096], P('shard')
- grad_cross_qkv: float32 [1024, 3072], P('shard')
- grad_cross_out: float32 [1024, 1024], P('shard')
- grad_cross_vec: float32 [4096], P('shard')
- grad_fc_in: float32 [1024, 8192], P('shard')
- grad_fc_out: float32 [8192, 1024], P('shard')
- grad_mlp_vec: float32 [10240], P('shard')
The draws below stay inside these ranges and needn't reach their ends.
Inputs may be any that keep to these rules, and one draw needn't show every extreme that they name: `pad_mask`: in each sequence of 1024 tokens the real tokens (1) come first and number 1024 - 1024 // 4 or more; the rest is padding (0).
All inputs are finite; a program needn't handle non-finite values.
Results may differ from the reference program's by a relative error of at most 0.02.
Values may be sent and summed in bfloat16 or wider, within the bound.
No kernel may reach another device: no remote copies, remote signals or barrier semaphores. Data moves between devices by JAX's collectives and lax.ppermute only.
A program may use at most 384 MiB of HBM per device.

```python
import math
import jax
import jax.numpy as jnp
import numpy as np
from jax import lax

D = 1024
HEADS = 16
HEAD_DIM = 64
FF = 8192
LEN = 1024
SRC_LEN = 1024
SEQS = 32
TOKENS = 32768


def draw_pad_mask(key, part):
    seq_count = TOKENS // LEN
    valid = jax.random.randint(key, (seq_count,), LEN - LEN // 4, LEN + 1).astype(jnp.int32)
    valid = valid.at[0].set(LEN - LEN // 4)
    places = jnp.arange(LEN, dtype=jnp.int32)
    return (places[None, :] < valid[:, None]).astype(jnp.int32).reshape(TOKENS)


def touch_ends(values, key, smallest, top_value):
    longest = values.shape.index(max(values.shape))
    spots = []
    for shift in (0, 1):
        where = [jax.random.randint(jax.random.fold_in(key, axis), (), 0, length) for axis, length in enumerate(values.shape)]
        where[longest] = (where[longest] + shift) % values.shape[longest]
        spots.append(tuple(where))
    return values.at[spots[0]].set(smallest).at[spots[1]].set(top_value)


def block_levels(stream_key, extent, split, least, largest):
    level = 1.0
    for dim, blocks in split:
        steps = jax.random.uniform(jax.random.fold_in(jax.random.fold_in(stream_key, 6), dim), (blocks,), jnp.float32, least / len(split), largest / len(split))
        level = level * jnp.repeat(jnp.exp(steps), extent[dim] // blocks).reshape((-1,) + (1,) * (len(extent) - 1 - dim))
    return level


def profile(number_of, total, limit, lean):
    weights = [(1 << 20) // math.isqrt(rank ** lean) + 1 for rank in range(2, number_of + 1)]
    rest, given = total - limit - (number_of - 1), [1] * (number_of - 1)
    while rest > 0:
        free = [i for i in range(number_of - 1) if given[i] < limit]
        whole, budget = sum([weights[i] for i in free]), rest
        for i in free:
            extra = min(limit - given[i], max(1, budget * weights[i] // whole), rest)
            given[i] = given[i] + extra
            rest = rest - extra
    return np.array([limit] + given)


def uneven(key, amount, total, most, slope):
    if amount == 2:
        one = jax.random.randint(key, (), max(1, total - most), min(most, total - 1) + 1)
        return jnp.stack([one, total - one])
    sizes = jnp.asarray(profile(amount, total, most, slope), jnp.int32)
    couples = (amount - 1) // 2
    source_of, taker = sizes[1:1 + 2 * couples:2], sizes[2:2 + 2 * couples:2]
    room = jnp.minimum(source_of - 1, most - taker)
    shifted = jax.random.randint(jax.random.fold_in(key, 1), (couples,), 0, 1 << 20) % (room + 1)
    sizes = sizes.at[1:1 + 2 * couples:2].set(source_of - shifted).at[2:2 + 2 * couples:2].set(taker + shifted)
    return sizes[jax.random.permutation(jax.random.fold_in(key, 2), amount)]


def scatter_about(stream_key, dims, scale, reach, pieces=(), kind=jnp.bfloat16):
    values = scale * jax.random.normal(stream_key, dims, jnp.float32)
    if pieces:
        values = values * block_levels(stream_key, dims, pieces, -0.22, 0.18)
    return jnp.clip(values, -reach, reach).astype(kind)


def setup_inputs(seed: int = 0) -> dict:
    key_of = jax.random.split(jax.random.key(seed), 17)
    return {
        "hidden": scatter_about(key_of[0], (TOKENS, D), 1.0, 6.0, ((0, 32),)),
        "segments": jnp.searchsorted(jnp.cumsum(uneven(key_of[1], TOKENS * 2 // LEN, TOKENS, LEN, 2)), jnp.arange(TOKENS), side="right").astype(jnp.int32),
        "pad_mask": draw_pad_mask(jax.random.fold_in(key_of[16], 71), 0),
        "encoder": scatter_about(key_of[3], (SEQS, SRC_LEN, D), 1.0, 6.0, ((0, 32),)),
        "src_len": touch_ends(jax.random.randint(key_of[4], (SEQS,), SRC_LEN // 4, SRC_LEN + 1), jax.random.fold_in(key_of[4], 1), SRC_LEN // 4, SRC_LEN).astype(jnp.int32),
        "grad_out": scatter_about(key_of[5], (TOKENS, D), 1.0, 6.0, ((0, 32),)),
        "ln_gain": jnp.clip(1.0 + 0.18 * jax.random.normal(key_of[6], (3, D), jnp.float32), 0.099609375, 1.8984375).astype(jnp.bfloat16),
        "self_qkv": scatter_about(key_of[7], (D, 3 * D), D ** -0.5, 0.1875, ((0, 8),)),
        "self_out": scatter_about(key_of[8], (D, D), (D // 4) ** -0.5, 0.375, ((0, 8),)),
        "self_vec": scatter_about(key_of[9], (4 * D,), 0.5, 3.0, ((0, 8),)),
        "cross_qkv": scatter_about(key_of[10], (D, 3 * D), D ** -0.5, 0.1875, ((0, 8),)),
        "cross_out": scatter_about(key_of[11], (D, D), (D // 4) ** -0.5, 0.375, ((0, 8),)),
        "cross_vec": scatter_about(key_of[12], (4 * D,), 0.5, 3.0, ((0, 8),)),
        "fc_in": scatter_about(key_of[13], (D, FF), D ** -0.5, 0.1875, ((0, 8),)),
        "fc_out": scatter_about(key_of[14], (FF, D), (FF // 2) ** -0.5, 0.09375, ((0, 8),)),
        "mlp_vec": scatter_about(key_of[15], (2 * D + FF,), 0.5, 3.0, ((0, 8),)),
    }


EPSILON = 1e-05
MASKED = -1e+30

@jax.custom_vjp
def low(v):
    return lax.optimization_barrier(v.astype(jnp.bfloat16)).astype(jnp.float32)

@jax.custom_vjp
def low_back(v):
    return v

def low_keep(v):
    return (low(v), None)

def low_pass(kept, grad):
    return (grad,)

def back_keep(v):
    return (v, None)

def back_low(kept, grad):
    return (low(grad),)
low.defvjp(low_keep, low_pass)
low_back.defvjp(back_keep, back_low)

def product(left, right):
    return jnp.dot(left, right, precision=lax.Precision.HIGHEST, preferred_element_type=jnp.float32)

def smooth_unit(values):
    return jax.nn.gelu(values, approximate=True)

def layer_norm(values, gain, shift):
    center = lax.optimization_barrier(jnp.mean(values, -1, keepdims=True))
    offset = values - center
    spread = lax.optimization_barrier(jnp.mean(offset * offset, -1, keepdims=True))
    return offset * lax.rsqrt(spread + EPSILON) * gain + shift

def attention(queries, key_rows, value_rows, allowed):
    q_heads = queries.reshape(queries.shape[0], HEADS, HEAD_DIM)
    k_heads = key_rows.reshape(key_rows.shape[0], HEADS, HEAD_DIM)
    v_heads = value_rows.reshape(value_rows.shape[0], HEADS, HEAD_DIM)
    scores = jnp.einsum('qhd,khd->hqk', q_heads, k_heads, precision=lax.Precision.HIGHEST, preferred_element_type=jnp.float32)
    masked_fill = jnp.full(scores.shape, MASKED, scores.dtype)
    scores = low_back(jnp.where(allowed[None], scores, masked_fill))
    row_max = lax.optimization_barrier(jnp.max(scores, -1, keepdims=True))
    exp_scores = jnp.exp(scores - row_max)
    weights_p = low(exp_scores / lax.optimization_barrier(jnp.sum(exp_scores, -1, keepdims=True)))
    mixed = jnp.einsum('hqk,khd->qhd', weights_p, v_heads, precision=lax.Precision.HIGHEST, preferred_element_type=jnp.float32)
    return mixed.reshape(queries.shape[0], HEADS * HEAD_DIM)

def forward(tokens, encoded, seg_ids, pad_ids, length, params):
    gains, qkv_one, out_one, vec_one, qkv_two, out_two, vec_two, fc_first, fc_second, vec_three = params
    normed_one = low(layer_norm(tokens, gains[0], vec_one[:D]))
    projected = product(normed_one, qkv_one)
    query_one = low(low_back((projected[:, :D] + vec_one[D:2 * D]) * 0.125))
    key_one = low(low_back(projected[:, D:2 * D]))
    value_one = low(low_back(projected[:, 2 * D:] + vec_one[2 * D:3 * D]))
    row_ids = jnp.arange(LEN, dtype=jnp.int32)[:, None]
    col_ids = jnp.arange(LEN, dtype=jnp.int32)[None, :]
    allowed_self = (col_ids <= row_ids) & (seg_ids[:, None] == seg_ids[None, :]) & ((pad_ids[None, :] == 1) | (col_ids == row_ids))
    attended_one = low(low_back(attention(query_one, key_one, value_one, allowed_self)))
    after_one = tokens + low_back(product(attended_one, out_one) + vec_one[3 * D:])
    normed_two = low(layer_norm(after_one, gains[1], vec_two[:D]))
    query_two = low(low_back((product(normed_two, qkv_two[:, :D]) + vec_two[D:2 * D]) * 0.125))
    kv_two = product(encoded, qkv_two[:, D:])
    key_two = low(low_back(kv_two[:, :D]))
    value_two = low(low_back(kv_two[:, D:] + vec_two[2 * D:3 * D]))
    src_ids = jnp.arange(SRC_LEN, dtype=jnp.int32)[None, :]
    allowed_cross = jnp.broadcast_to(src_ids < length.astype(jnp.int32), (LEN, SRC_LEN))
    attended_two = low(low_back(attention(query_two, key_two, value_two, allowed_cross)))
    after_two = after_one + low_back(product(attended_two, out_two) + vec_two[3 * D:])
    normed_three = low(layer_norm(after_two, gains[2], vec_three[:D]))
    pre_act = low_back(product(normed_three, fc_first) + vec_three[2 * D:])
    activated = low(smooth_unit(pre_act))
    return after_two + low_back(product(activated, fc_second) + vec_three[D:2 * D])

def reference(hidden, segments, pad_mask, encoder, src_len, grad_out, ln_gain, self_qkv, self_out, self_vec, cross_qkv, cross_out, cross_vec, fc_in, fc_out, mlp_vec):
    params = tuple((weight_array.astype(jnp.float32) for weight_array in (ln_gain, self_qkv, self_out, self_vec, cross_qkv, cross_out, cross_vec, fc_in, fc_out, mlp_vec)))
    seq_count = TOKENS // LEN
    inputs_all = (hidden.astype(jnp.float32).reshape(seq_count, LEN, D), segments.astype(jnp.int32).reshape(seq_count, LEN), pad_mask.astype(jnp.int32).reshape(seq_count, LEN), encoder.astype(jnp.float32), src_len.astype(jnp.int32), grad_out.astype(jnp.float32).reshape(seq_count, LEN, D))

    def advance(totals, element):
        tokens, seg_ids, pad_ids, encoded, length, cotangent = element

        def run_layer(tokens, encoded, params):
            return forward(tokens, encoded, seg_ids, pad_ids, length, params)
        result, pullback = jax.vjp(run_layer, tokens, encoded, params)
        grad_tokens, grad_encoded, grad_params = pullback(cotangent)
        totals = jax.tree.map(jnp.add, totals, grad_params)
        return (totals, (result.astype(jnp.bfloat16), grad_tokens.astype(jnp.bfloat16), grad_encoded.astype(jnp.bfloat16)))
    zeroes = jax.tree.map(jnp.zeros_like, params)
    sums, (results, grad_rows, grad_states) = lax.scan(advance, zeroes, inputs_all)
    factor = 1.0 / math.sqrt(TOKENS)
    grads = jax.tree.map(lambda total: total * factor, sums)
    return (results.reshape(TOKENS, D), grad_rows.reshape(TOKENS, D), grad_states, grads[0], grads[1], grads[2], grads[3], grads[4], grads[5], grads[6], grads[7], grads[8], grads[9])
```

```python
import functools
import math

import jax
import jax.numpy as jnp
from jax import lax
from jax.experimental import pallas as pl
from jax.experimental.pallas import tpu as pltpu
from jax.sharding import PartitionSpec as P

HEADS = 16
HEAD_DIM = 64
EPSILON = 1e-05
MASKED = -1e30
GELU_A = math.sqrt(2.0 / math.pi)
GELU_B = GELU_A * 0.044715

D = 1024
ROWS = 1024
GROUP = 256
GROUPS = 4
PIECES = 8
QBLOCK = 512
KBLOCK = 256
TILE = 512
F32 = jnp.float32
BF16 = jnp.bfloat16
VMEM_LIMIT = 62 * 1024 * 1024


def dot(left, right):
    return jnp.dot(left, right, preferred_element_type=F32)


def dot_t(left, right):
    return lax.dot_general(left, right, (((1,), (1,)), ((), ())), preferred_element_type=F32)


def dot_a(left, right):
    return lax.dot_general(left, right, (((0,), (0,)), ((), ())), preferred_element_type=F32)


def normalize(values):
    center = jnp.mean(values, -1, keepdims=True)
    offset = values - center
    scale_inv = lax.rsqrt(jnp.mean(offset * offset, -1, keepdims=True) + EPSILON)
    return offset * scale_inv, scale_inv


def norm_back(grad, values, gain):
    normed, scale_inv = normalize(values)
    scaled = grad * gain
    back = scale_inv * (
        scaled
        - jnp.mean(scaled, -1, keepdims=True)
        - normed * jnp.mean(scaled * normed, -1, keepdims=True)
    )
    return back, jnp.sum(grad * normed, 0, keepdims=True), jnp.sum(grad, 0, keepdims=True)


def split_three(values):
    high = values.astype(BF16)
    rest = values - high.astype(F32)
    middle = rest.astype(BF16)
    return high, middle, (rest - middle.astype(F32)).astype(BF16)


def place(me, rank):
    return lax.bitwise_xor(me, rank)


def qkv_copies(me, group, first, second, weights, sems):
    copies = []
    slot = group % 2
    for rank in range(PIECES):
        rows = pl.ds(pl.multiple_of(place(me, rank) * 128, 128), 128)
        for index, (piece, offset) in enumerate(
            ((first[rank], 0), (first[rank], D), (second[rank], 0))
        ):
            source = pl.ds(pl.multiple_of(offset + group * GROUP, GROUP), GROUP)
            target = pl.ds(index * GROUP, GROUP)
            copies.append(
                pltpu.make_async_copy(
                    piece.at[:, source],
                    weights.at[slot, rows, target],
                    sems.at[slot, rank * 3 + index],
                )
            )
    return copies


def out_copies(me, second, out_weights, sems):
    copies = []
    for rank in range(PIECES):
        rows = pl.ds(pl.multiple_of(place(me, rank) * 128, 128), 128)
        copies.append(
            pltpu.make_async_copy(
                second[rank].at[:, pl.ds(D, D)], out_weights.at[rows, :], sems.at[rank]
            )
        )
    return copies


def start_all(copies):
    for copy in copies:
        copy.start()


def wait_all(copies):
    for copy in copies:
        copy.wait()


def build_self_bias(seg_col, seg_row, pad_row, bias):
    for first in range(0, ROWS, QBLOCK):
        count = first + QBLOCK
        rows = first + lax.broadcasted_iota(jnp.int32, (QBLOCK, count), 0)
        cols = lax.broadcasted_iota(jnp.int32, (QBLOCK, count), 1)
        same = seg_col[first : first + QBLOCK, :] == seg_row[:, :count]
        real = (pad_row[:, :count] == 1) | (cols == rows)
        allowed = (cols <= rows) & same & real
        bias[first : first + QBLOCK, :count] = jnp.where(allowed, 0.0, MASKED)


def lanes_of(half):
    lane = lax.broadcasted_iota(jnp.int32, (1, 128), 1)
    mine = (lane < 64) if half == 0 else (lane >= 64)
    return lane, mine, (64 if half == 0 else 0)


def key_mask(shape, length):
    rows = lax.broadcasted_iota(jnp.int32, shape, 0)
    return jnp.where(rows < length, 0.0, MASKED).astype(BF16)


def forward_pair(query, key, value, length, bias, out_ref, log_ref, pair, causal):
    lane, _, _ = lanes_of(0)
    columns = slice(pair * 128, pair * 128 + 128)
    logs = [[], []]
    for first in range(0, ROWS, QBLOCK):
        count = first + QBLOCK if causal else key.shape[0]
        outs = []
        for half in range(2):
            _, mine, extra = lanes_of(half)
            q_block = query[first : first + QBLOCK]
            if causal:
                q_ext = jnp.where(mine, q_block, jnp.zeros_like(q_block))
                scores = dot_t(q_ext, key[:count]) + bias[first : first + QBLOCK, :count]
            else:
                q_ext = jnp.where(mine, q_block, (lane == extra).astype(BF16))
                k_ext = jnp.where(lane == extra, key_mask(key.shape, length), key)
                scores = dot_t(q_ext, k_ext)
            row_max = jnp.max(scores, 1, keepdims=True)
            weights = jnp.exp(scores - row_max).astype(BF16)
            v_ext = jnp.where(mine, value[:count], jnp.ones_like(value[:count]))
            mixed = dot(weights, v_ext)
            total = mixed[:, extra : extra + 1]
            outs.append((mixed, total))
            log_ref[0, first : first + QBLOCK, 2 * pair + half : 2 * pair + half + 1] = (
                row_max + jnp.log(total)
            )
        numerator = jnp.where(lane < 64, outs[0][0], outs[1][0])
        denominator = jnp.where(lane < 64, outs[0][1], outs[1][1])
        out_ref[first : first + QBLOCK, columns] = (numerator / denominator).astype(BF16)


def attend_forward_body(cross, *refs):
    it = iter(refs)
    scalars = next(it)
    x_ref = next(it)
    if cross:
        enc_ref = next(it)
    else:
        seg_col, seg_row, pad_row = next(it), next(it), next(it)
    gain, shift, out_bias, q_bias, v_bias = (next(it) for _ in range(5))
    first = [next(it) for _ in range(PIECES)]
    second = [next(it) for _ in range(PIECES)]
    x_out, q_ref, k_ref, v_ref, o_ref, log_ref = (next(it) for _ in range(6))
    a_ref, weights, out_weights, sems, out_sems = (next(it) for _ in range(5))
    bias = None if cross else next(it)
    group = pl.program_id(0)
    me = scalars[0]
    length = scalars[1]

    @pl.when(group == 0)
    def _():
        start_all(qkv_copies(me, 0, first, second, weights, sems))
        start_all(out_copies(me, second, out_weights, out_sems))
        values = x_ref[...].astype(F32)
        normed, _ = normalize(values)
        a_ref[...] = (normed * gain[...] + shift[...]).astype(BF16)
        x_out[...] = values + out_bias[...]
        if not cross:
            build_self_bias(seg_col, seg_row, pad_row, bias)

    @pl.when(group < GROUPS - 1)
    def _():
        start_all(qkv_copies(me, group + 1, first, second, weights, sems))

    wait_all(qkv_copies(me, group, first, second, weights, sems))

    def block(index):
        return weights[group % 2, :, index * GROUP : (index + 1) * GROUP]

    kv_rows = enc_ref[...] if cross else a_ref[...]
    q_ref[...] = ((dot(a_ref[...], block(0)) + q_bias[...]) * 0.125).astype(BF16)
    k_ref[...] = dot(kv_rows, block(1)).astype(BF16)
    v_ref[...] = (dot(kv_rows, block(2)) + v_bias[...]).astype(BF16)
    for pair in range(2):
        columns = slice(pair * 128, pair * 128 + 128)
        forward_pair(
            q_ref[:, columns],
            k_ref[:, columns],
            v_ref[:, columns],
            length,
            bias,
            o_ref,
            log_ref,
            pair,
            not cross,
        )

    @pl.when(group == 0)
    def _():
        wait_all(out_copies(me, second, out_weights, out_sems))

    rows = pl.ds(pl.multiple_of(group * GROUP, GROUP), GROUP)
    x_out[...] += dot(o_ref[...], out_weights[rows, :])


def whole(shape):
    zeros = (0,) * len(shape)
    return pl.BlockSpec(shape, lambda *_: zeros, pipeline_mode=pl.Buffered(1))


def whole_out(shape):
    zeros = (0,) * len(shape)
    return pl.BlockSpec(shape, lambda *_: zeros, pipeline_mode=pl.Buffered(1))


def group_block(rows=ROWS):
    return pl.BlockSpec((rows, GROUP), lambda g, s: (0, g))


ANY = pl.BlockSpec(memory_space=pl.ANY)


def cost(flops, nbytes, exps=0):
    return pl.CostEstimate(flops=int(flops), bytes_accessed=int(nbytes), transcendentals=int(exps))


def attend_forward(scalars, x, extras, vectors, first, second):
    cross = len(extras) == 1
    gain, shift, out_bias, q_bias, v_bias = vectors
    if cross:
        extra_specs = [whole((ROWS, D))]
    else:
        extra_specs = [whole((ROWS, 1)), whole((1, ROWS)), whole((1, ROWS))]
    scratch = [
        pltpu.VMEM((ROWS, D), BF16),
        pltpu.VMEM((2, D, 3 * GROUP), BF16),
        pltpu.VMEM((D, D), BF16),
        pltpu.SemaphoreType.DMA((2, 3 * PIECES)),
        pltpu.SemaphoreType.DMA((PIECES,)),
    ]
    if not cross:
        scratch.append(pltpu.VMEM((ROWS, ROWS), F32))
    return pl.pallas_call(
        functools.partial(attend_forward_body, cross),
        grid_spec=pltpu.PrefetchScalarGridSpec(
            num_scalar_prefetch=1,
            grid=(GROUPS,),
            in_specs=[whole((ROWS, D))]
            + extra_specs
            + [whole((1, D))] * 3
            + [group_block(1)] * 2
            + [ANY] * (2 * PIECES),
            out_specs=[whole_out((ROWS, D))]
            + [group_block()] * 4
            + [pl.BlockSpec((1, ROWS, 4), lambda g, s: (g, 0, 0))],
            scratch_shapes=scratch,
        ),
        out_shape=[jax.ShapeDtypeStruct((ROWS, D), F32)]
        + [jax.ShapeDtypeStruct((ROWS, D), BF16)] * 4
        + [jax.ShapeDtypeStruct((GROUPS, ROWS, 4), F32)],
        compiler_params=pltpu.CompilerParams(vmem_limit_bytes=VMEM_LIMIT),
        cost_estimate=cost(2 * ROWS * D * D * (4 + 8), 30e6, HEADS * ROWS * ROWS),
        name="cross_forward" if cross else "self_forward",
    )(scalars, x, *extras, gain, shift, out_bias, q_bias, v_bias, *first, *second)


def backward_pair(refs, go_ref, length, bias, accs, pair, causal):
    q_ref, k_ref, v_ref, o_ref, log_ref = refs
    dq_ref, dk_ref, dv_ref, dk_acc, dv_acc = accs
    columns = slice(pair * 128, pair * 128 + 128)
    query, key, value = q_ref[:, columns], k_ref[:, columns], v_ref[:, columns]
    go = go_ref[:, columns]
    q_turned, go_turned = query.T, go.T
    product = go.astype(F32) * o_ref[:, columns].astype(F32)
    zeros = jnp.zeros_like(query)
    q_ext, go_ext, k_ext, v_ext, k_own = [], [], [], [], []
    for half in range(2):
        lane, mine, extra = lanes_of(half)
        delta = jnp.sum(jnp.where(mine, product, 0.0), 1, keepdims=True)
        logs = log_ref[0, :, 2 * pair + half : 2 * pair + half + 1]
        k_own.append(jnp.where(mine, key, zeros))

        def with_rows(base, column, last):
            high, middle, low = split_three(-column)
            filled = jnp.where(lane == extra, high, jnp.where(lane == extra + 1, middle, zeros))
            filled = jnp.where(lane == extra + 2, low, filled)
            filled = jnp.where(lane == extra + 3, last, filled)
            return jnp.where(mine, base, filled)

        ones = ((lane >= extra) & (lane < extra + 3)).astype(BF16)
        one = jnp.ones_like(query)
        q_ext.append(with_rows(query, logs, zeros if causal else one))
        go_ext.append(with_rows(go, delta, zeros))
        keys = jnp.where(mine, key, ones)
        if not causal:
            keys = jnp.where(lane == extra + 3, key_mask(key.shape, length), keys)
        k_ext.append(keys)
        v_ext.append(jnp.where(mine, value, ones))
    last_first = ROWS - KBLOCK
    for first in range(last_first, -1, -KBLOCK):
        rows = slice(first, first + KBLOCK)
        count = first + KBLOCK if causal else key.shape[0]
        grads_q = []
        for half in range(2):
            scores = dot_t(q_ext[half][rows], k_ext[half][:count])
            if causal:
                scores = scores + bias[rows, :count]
            weights = jnp.exp(scores)
            grad_weights = dot_t(go_ext[half][rows], v_ext[half][:count])
            grad_scores = (weights * grad_weights).astype(BF16)
            grads_q.append(dot(grad_scores, k_own[half][:count]))
            dims = slice(64 * half, 64 * half + 64)
            grad_value = dot(go_turned[dims, rows], weights.astype(BF16))
            grad_key = dot(q_turned[dims, rows], grad_scores)
            if first == last_first:
                dv_acc[dims, :] = grad_value
                dk_acc[dims, :] = grad_key
            else:
                dv_acc[dims, :count] += grad_value
                dk_acc[dims, :count] += grad_key
        dq_ref[rows, columns] = (grads_q[0] + grads_q[1]).astype(BF16) * 0.125
    dk_ref[:, columns] = dk_acc[...].astype(BF16).T
    dv_ref[:, columns] = dv_acc[...].astype(BF16).T


def scatter_rows(me, value, holder, keep, send, columns, height):
    holder[...] = value.astype(BF16).reshape(PIECES, height, value.shape[1])
    for slot in range(PIECES // 2):
        pair = place(slot, me // 2) * 2
        keep[slot, :, columns] = holder[pair + me % 2]
        send[slot, :, columns] = holder[pair + (1 - me % 2)]


def attend_backward_body(cross, *refs):
    it = iter(refs)
    scalars = next(it)
    gx_hbm, x_hbm = next(it), next(it)
    enc_t = next(it) if cross else None
    if not cross:
        seg_col, seg_row, pad_row = next(it), next(it), next(it)
    gain, shift = next(it), next(it)
    q_ref, k_ref, v_ref, o_ref, log_ref = (next(it) for _ in range(5))
    first = [next(it) for _ in range(PIECES)]
    second = [next(it) for _ in range(PIECES)]
    gx_out = next(it)
    genc_out = next(it) if cross else None
    keep_a, send_a, keep_b, send_b = (next(it) for _ in range(4))
    q_sum, v_sum, b_sum, gain_sum, shift_sum = (next(it) for _ in range(5))
    gx, x_ref, a_t, gb, da, weights, out_weights, sems, out_sems, sem = (
        next(it) for _ in range(10)
    )
    go, dq, dk, dv, dk_acc, dv_acc, holder, holder_out = (next(it) for _ in range(8))
    denc = next(it) if cross else None
    bias = None if cross else next(it)
    result = None if cross else next(it)
    group = pl.program_id(0)
    me = scalars[0]
    length = scalars[1]

    @pl.when(group == 0)
    def _():
        load_x = pltpu.make_async_copy(x_hbm, x_ref, sem.at[0])
        load_gx = pltpu.make_async_copy(gx_hbm, gx, sem.at[1])
        load_x.start()
        load_gx.start()
        start_all(out_copies(me, second, out_weights, out_sems))
        start_all(qkv_copies(me, 0, first, second, weights, sems))
        load_x.wait()
        normed, _ = normalize(x_ref[...].astype(F32))
        a_t[...] = (normed * gain[...] + shift[...]).astype(BF16).T
        load_gx.wait()
        gb[...] = gx[...].astype(BF16)
        b_sum[...] = jnp.sum(gb[...].astype(F32), 0, keepdims=True)
        if not cross:
            build_self_bias(seg_col, seg_row, pad_row, bias)
        wait_all(out_copies(me, second, out_weights, out_sems))

    @pl.when(group < GROUPS - 1)
    def _():
        start_all(qkv_copies(me, group + 1, first, second, weights, sems))

    rows = pl.ds(pl.multiple_of(group * GROUP, GROUP), GROUP)
    go[...] = dot_t(gb[...], out_weights[rows, :]).astype(BF16)
    grad_out = dot(o_ref[...].T, gb[...])
    holder_out[...] = grad_out.astype(BF16).reshape(2, 128, D)
    slot = place(group, me // 2)
    keep_b[slot, :, D : 2 * D] = holder_out[me % 2]
    send_b[slot, :, D : 2 * D] = holder_out[1 - me % 2]
    for pair in range(2):
        backward_pair(
            (q_ref, k_ref, v_ref, o_ref, log_ref),
            go,
            length,
            bias,
            (dq, dk, dv, dk_acc, dv_acc),
            pair,
            not cross,
        )
    wait_all(qkv_copies(me, group, first, second, weights, sems))

    def columns_of(index):
        return pl.ds(pl.multiple_of(index * D + group * GROUP, GROUP), GROUP)

    kv_t = enc_t if cross else a_t
    scatter_rows(me, dot(a_t[...], dq[...]), holder, keep_a, send_a, columns_of(0), 128)
    scatter_rows(me, dot(kv_t[...], dk[...]), holder, keep_a, send_a, columns_of(1), 128)
    scatter_rows(me, dot(kv_t[...], dv[...]), holder, keep_b, send_b, columns_of(0), 128)
    q_sum[...] = jnp.sum(dq[...].astype(F32), 0, keepdims=True)
    v_sum[...] = jnp.sum(dv[...].astype(F32), 0, keepdims=True)
    slot = group % 2
    from_q = dot_t(dq[...], weights[slot, :, 0:GROUP])
    from_kv = dot_t(dk[...], weights[slot, :, GROUP : 2 * GROUP]) + dot_t(
        dv[...], weights[slot, :, 2 * GROUP : 3 * GROUP]
    )
    if not cross:
        from_q = from_q + from_kv

    @pl.when(group == 0)
    def _():
        da[...] = from_q
        if cross:
            denc[...] = from_kv

    @pl.when(group > 0)
    def _():
        da[...] += from_q
        if cross:
            denc[...] += from_kv

    @pl.when(group == GROUPS - 1)
    def _():
        back, gain_grad, shift_grad = norm_back(da[...], x_ref[...].astype(F32), gain[...])
        gain_sum[...] = gain_grad
        shift_sum[...] = shift_grad
        if cross:
            gx[...] = gx[...] + back
            store = pltpu.make_async_copy(gx, gx_out, sem.at[0])
            store.start()
            gb[...] = denc[...].astype(BF16)
            store_enc = pltpu.make_async_copy(gb, genc_out, sem.at[1])
            store_enc.start()
            store_enc.wait()
        else:
            result[...] = (gx[...] + back).astype(BF16)
            store = pltpu.make_async_copy(result, gx_out, sem.at[0])
            store.start()
        store.wait()


def attend_backward(scalars, gx, x, extras, vectors, saved, first, second):
    cross = len(extras) == 1
    gain, shift = vectors
    if cross:
        extra_specs = [whole((D, ROWS))]
    else:
        extra_specs = [whole((ROWS, 1)), whole((1, ROWS)), whole((1, ROWS))]
    half = PIECES // 2
    scratch = [
        pltpu.VMEM((ROWS, D), F32),
        pltpu.VMEM((ROWS, D), x.dtype),
        pltpu.VMEM((D, ROWS), BF16),
        pltpu.VMEM((ROWS, D), BF16),
        pltpu.VMEM((ROWS, D), F32),
        pltpu.VMEM((2, D, 3 * GROUP), BF16),
        pltpu.VMEM((D, D), BF16),
        pltpu.SemaphoreType.DMA((2, 3 * PIECES)),
        pltpu.SemaphoreType.DMA((PIECES,)),
        pltpu.SemaphoreType.DMA((2,)),
        pltpu.VMEM((ROWS, GROUP), BF16),
        pltpu.VMEM((ROWS, GROUP), BF16),
        pltpu.VMEM((ROWS, GROUP), BF16),
        pltpu.VMEM((ROWS, GROUP), BF16),
        pltpu.VMEM((128, ROWS), F32),
        pltpu.VMEM((128, ROWS), F32),
        pltpu.VMEM((PIECES, 128, GROUP), BF16),
        pltpu.VMEM((2, 128, D), BF16),
    ]
    out_shape = [jax.ShapeDtypeStruct((ROWS, D), F32 if cross else BF16)]
    out_specs = [ANY]
    if cross:
        scratch.append(pltpu.VMEM((ROWS, D), F32))
        out_shape.append(jax.ShapeDtypeStruct((ROWS, D), BF16))
        out_specs.append(ANY)
    else:
        scratch.append(pltpu.VMEM((ROWS, ROWS), F32))
        scratch.append(pltpu.VMEM((ROWS, D), BF16))
    out_shape += [jax.ShapeDtypeStruct((half, 128, 2 * D), BF16)] * 4
    out_specs += [whole_out((half, 128, 2 * D))] * 4
    out_shape += [jax.ShapeDtypeStruct((1, D), F32)] * 5
    out_specs += [group_block(1)] * 2 + [whole_out((1, D))] * 3
    return pl.pallas_call(
        functools.partial(attend_backward_body, cross),
        grid_spec=pltpu.PrefetchScalarGridSpec(
            num_scalar_prefetch=1,
            grid=(GROUPS,),
            in_specs=[ANY, ANY]
            + extra_specs
            + [whole((1, D))] * 2
            + [group_block()] * 4
            + [pl.BlockSpec((1, ROWS, 4), lambda g, s: (g, 0, 0))]
            + [ANY] * (2 * PIECES),
            out_specs=out_specs,
            scratch_shapes=scratch,
        ),
        out_shape=out_shape,
        compiler_params=pltpu.CompilerParams(vmem_limit_bytes=VMEM_LIMIT),
        cost_estimate=cost(2 * ROWS * D * D * (8 + 20), 50e6, HEADS * ROWS * ROWS),
        name="cross_backward" if cross else "self_backward",
    )(scalars, gx, x, *extras, gain, shift, *saved, *first, *second)


def mlp_body(first_call, last_call, tiles, *refs):
    it = iter(refs)
    scalars = next(it)
    a_ref, a_t, go = next(it), next(it), next(it)
    b1 = next(it)
    acc_in = None if first_call else (next(it), next(it))
    if last_call:
        x_hbm, out_bias, gain = next(it), next(it), next(it)
    first = [next(it) for _ in range(PIECES)]
    second = [next(it) for _ in range(PIECES)]
    keep_a, send_a, keep_b, send_b, b1_sum = (next(it) for _ in range(5))
    acc_out = (next(it), next(it))
    if last_call:
        gain_sum, shift_sum = next(it), next(it)
    out_acc, da_acc, w1, w2, sems1, sems2, sem, holder, holder2 = (next(it) for _ in range(9))
    if last_call:
        x_ref, result = next(it), next(it)
    step = pl.program_id(0)
    me = scalars[0]
    height = TILE // 2

    def first_copies(tile, slot):
        copies = []
        for rank in range(PIECES):
            rows = pl.ds(pl.multiple_of(place(me, rank) * 128, 128), 128)
            columns = pl.ds(pl.multiple_of(tile * TILE, TILE), TILE)
            copies.append(
                pltpu.make_async_copy(
                    first[rank].at[:, columns], w1.at[slot, rows, :], sems1.at[slot, rank]
                )
            )
        return copies

    def second_copies():
        copies = []
        for rank in range(PIECES):
            rows = pl.ds(pl.multiple_of(place(me, rank) * height, height), height)
            copies.append(pltpu.make_async_copy(second[rank], w2.at[rows, :], sems2.at[rank]))
        return copies

    def acc_copies():
        return [
            pltpu.make_async_copy(acc_in[0], out_acc, sem.at[0]),
            pltpu.make_async_copy(acc_in[1], da_acc, sem.at[1]),
        ]

    slot = step % 2

    @pl.when(step == 0)
    def _():
        start_all(first_copies(0, 0))
        start_all(second_copies())
        if first_call:
            out_acc[...] = jnp.zeros_like(out_acc)
            da_acc[...] = jnp.zeros_like(da_acc)
        else:
            start_all(acc_copies())
        if last_call:
            pltpu.make_async_copy(x_hbm, x_ref, sem.at[2]).start()
        wait_all(second_copies())
        if not first_call:
            wait_all(acc_copies())

    @pl.when(step < tiles - 1)
    def _():
        start_all(first_copies(step + 1, 1 - slot))

    wait_all(first_copies(step, slot))
    w1_tile = w1[slot]
    w2_tile = w2[pl.ds(pl.multiple_of(step * TILE, TILE), TILE), :]
    unit = dot(a_ref[...], w1_tile) + b1[...]
    square = unit * unit
    bent = jnp.tanh(unit * (GELU_A + GELU_B * square))
    halved = 0.5 * unit
    active = (halved + halved * bent).astype(BF16)
    slope = 0.5 + 0.5 * bent + halved * (1.0 - bent * bent) * (GELU_A + 3.0 * GELU_B * square)
    grad_unit = (dot_t(go[...], w2_tile) * slope).astype(BF16)
    out_acc[...] += dot(active, w2_tile)
    holder2[...] = dot_a(active, go[...]).astype(BF16).reshape(2, height, D)
    keep_b[0] = holder2[me % 2]
    send_b[0] = holder2[1 - me % 2]
    b1_sum[...] = jnp.sum(grad_unit.astype(F32), 0, keepdims=True)
    scatter_rows(me, dot(a_t[...], grad_unit), holder, keep_a, send_a, slice(None), 128)
    da_acc[...] += dot_t(grad_unit, w1_tile)

    @pl.when(step == tiles - 1)
    def _():
        if last_call:
            pltpu.make_async_copy(x_hbm, x_ref, sem.at[2]).wait()
            values = x_ref[...]
            result[...] = (values + out_acc[...] + out_bias[...]).astype(BF16)
            store_out = pltpu.make_async_copy(result, acc_out[0], sem.at[0])
            store_out.start()
            back, gain_grad, shift_grad = norm_back(da_acc[...], values, gain[...])
            gain_sum[...] = gain_grad
            shift_sum[...] = shift_grad
            da_acc[...] = go[...].astype(F32) + back
        else:
            store_out = pltpu.make_async_copy(out_acc, acc_out[0], sem.at[0])
            store_out.start()
        store = pltpu.make_async_copy(da_acc, acc_out[1], sem.at[1])
        store.start()
        store_out.wait()
        store.wait()


def mlp_chunk(scalars, a, a_t, go, b1, acc, last, first, second):
    width = first[0].shape[1]
    tiles = width // TILE
    first_call, last_call = acc is None, last is not None
    half = PIECES // 2
    height = TILE // 2
    operands = [a, a_t, go, b1]
    in_specs = [whole((ROWS, D)), whole((D, ROWS)), whole((ROWS, D))]
    in_specs.append(pl.BlockSpec((1, TILE), lambda i, s: (0, i)))
    if not first_call:
        operands += list(acc)
        in_specs += [ANY, ANY]
    if last_call:
        operands += list(last)
        in_specs += [ANY, whole((1, D)), whole((1, D))]
    grad_a = pl.BlockSpec((half, 128, TILE), lambda i, s: (0, 0, i))
    grad_b = pl.BlockSpec((1, height, D), lambda i, s: (lax.bitwise_xor(i, s[0] // 2), 0, 0))
    out_specs = [grad_a, grad_a, grad_b, grad_b, pl.BlockSpec((1, TILE), lambda i, s: (0, i))]
    out_shape = (
        [jax.ShapeDtypeStruct((half, 128, width), BF16)] * 2
        + [jax.ShapeDtypeStruct((half, height, D), BF16)] * 2
        + [jax.ShapeDtypeStruct((1, width), F32)]
        + [jax.ShapeDtypeStruct((ROWS, D), BF16 if last_call else F32)]
        + [jax.ShapeDtypeStruct((ROWS, D), F32)]
    )
    out_specs += [ANY, ANY]
    if last_call:
        out_shape += [jax.ShapeDtypeStruct((1, D), F32)] * 2
        out_specs += [whole_out((1, D))] * 2
    scratch = [
        pltpu.VMEM((ROWS, D), F32),
        pltpu.VMEM((ROWS, D), F32),
        pltpu.VMEM((2, D, TILE), BF16),
        pltpu.VMEM((width, D), BF16),
        pltpu.SemaphoreType.DMA((2, PIECES)),
        pltpu.SemaphoreType.DMA((PIECES,)),
        pltpu.SemaphoreType.DMA((3,)),
        pltpu.VMEM((PIECES, 128, TILE), BF16),
        pltpu.VMEM((2, height, D), BF16),
    ]
    if last_call:
        scratch += [pltpu.VMEM((ROWS, D), F32), pltpu.VMEM((ROWS, D), BF16)]
    return pl.pallas_call(
        functools.partial(mlp_body, first_call, last_call, tiles),
        grid_spec=pltpu.PrefetchScalarGridSpec(
            num_scalar_prefetch=1,
            grid=(tiles,),
            in_specs=in_specs + [ANY] * (2 * PIECES),
            out_specs=out_specs,
            scratch_shapes=scratch,
        ),
        out_shape=out_shape,
        compiler_params=pltpu.CompilerParams(vmem_limit_bytes=VMEM_LIMIT),
        cost_estimate=cost(6 * 2 * ROWS * D * width, 30e6, ROWS * width),
        name="mlp",
    )(scalars, *operands, *first, *second)


def norm_turn_body(x_ref, gain, shift, a_ref, a_t):
    normed, _ = normalize(x_ref[...].astype(F32))
    values = (normed * gain[...] + shift[...]).astype(BF16)
    a_ref[...] = values
    a_t[...] = values.T


def norm_turn(x, gain, shift):
    return pl.pallas_call(
        norm_turn_body,
        out_shape=[
            jax.ShapeDtypeStruct((ROWS, D), BF16),
            jax.ShapeDtypeStruct((D, ROWS), BF16),
        ],
        compiler_params=pltpu.CompilerParams(vmem_limit_bytes=VMEM_LIMIT),
        name="norm_turn",
    )(x, gain, shift)


CHUNKS = 4


def gather_vectors(ln_gain, self_vec, cross_vec, mlp_vec):
    sizes = [3 * ln_gain.shape[1], self_vec.shape[0], cross_vec.shape[0], mlp_vec.shape[0]]
    packed = jnp.concatenate([ln_gain.reshape(-1), self_vec, cross_vec, mlp_vec])
    every = lax.all_gather(packed, "shard").astype(F32)
    ends = [sum(sizes[: i + 1]) for i in range(4)]
    gains = every[:, : ends[0]].reshape(-1, 3, ln_gain.shape[1]).transpose(1, 0, 2)
    gains = gains.reshape(3, 1, D)
    return [gains] + [every[:, a:b].reshape(1, -1) for a, b in zip(ends[:3], ends[1:])]


def cut_rows(full):
    rows = full.shape[0] // PIECES
    return [full[rows * r : rows * (r + 1)] for r in range(PIECES)]


def join_pieces(keep, send):
    return jnp.stack([keep, send], 1).reshape(PIECES, *keep.shape[1:])


def summed(value):
    shard = lax.psum_scatter(value.astype(BF16), "shard", scatter_dimension=0, tiled=True)
    return lax.psum(shard, "rep").astype(F32)


def per_device(
    hidden,
    segments,
    pad_mask,
    encoder,
    src_len,
    grad_out,
    ln_gain,
    self_qkv,
    self_out,
    self_vec,
    cross_qkv,
    cross_out,
    cross_vec,
    fc_in,
    fc_out,
    mlp_vec,
):
    shards = lax.axis_size("shard")
    factor = 1.0 / math.sqrt(ROWS * lax.axis_size("rep") * shards)
    encoded = encoder.reshape(ROWS, D)
    enc_t = encoded.T
    gains, vec_one, vec_two, vec_three = gather_vectors(ln_gain, self_vec, cross_vec, mlp_vec)
    me = jnp.int32(0)
    scalars = jnp.stack([me, src_len[0]])

    def gather(value):
        return lax.all_gather(value, "shard", axis=0, tiled=True)

    def attention_weights(qkv, out):
        both = gather(jnp.concatenate([qkv, out], 1))
        return cut_rows(both[:, : 2 * D]), cut_rows(both[:, 2 * D :])

    first_one, second_one = attention_weights(self_qkv, self_out)
    first_two, second_two = attention_weights(cross_qkv, cross_out)
    full_in, full_out = gather(fc_in), gather(fc_out)
    ff = full_in.shape[1]
    step = ff // PIECES // CHUNKS
    pieces_in = full_in.reshape(D, PIECES, CHUNKS, step)
    pieces_out = full_out.reshape(PIECES, CHUNKS, step, D)
    bias_in = vec_three[:, 2 * D :].reshape(PIECES, CHUNKS, step)

    masks = (segments.reshape(ROWS, 1), segments.reshape(1, ROWS), pad_mask.reshape(1, ROWS))

    def part(vector, index):
        return vector[:, index * D : (index + 1) * D]

    x_one, *saved_one = attend_forward(
        scalars,
        hidden,
        masks,
        (gains[0], part(vec_one, 0), part(vec_one, 3), part(vec_one, 1), part(vec_one, 2)),
        first_one,
        second_one,
    )
    x_two, *saved_two = attend_forward(
        scalars,
        x_one,
        (encoded,),
        (gains[1], part(vec_two, 0), part(vec_two, 3), part(vec_two, 1), part(vec_two, 2)),
        first_two,
        second_two,
    )
    normed, normed_t = norm_turn(x_two, gains[2], part(vec_three, 0))
    acc = None
    grads_in, grads_out, sums_in = [], [], []
    for chunk in range(CHUNKS):
        last = chunk == CHUNKS - 1
        keep_a, send_a, keep_b, send_b, b1_sum, *acc = mlp_chunk(
            scalars,
            normed,
            normed_t,
            grad_out,
            bias_in[:, chunk].reshape(1, -1),
            acc,
            (x_two, part(vec_three, 1), gains[2]) if last else None,
            cut_rows(pieces_in[:, :, chunk].reshape(D, -1)),
            [pieces_out[r, chunk] for r in range(PIECES)],
        )
        grads_in.append(join_pieces(keep_a, send_a).reshape(D, PIECES, 1, step))
        grads_out.append(join_pieces(keep_b, send_b).reshape(PIECES, 1, step, D))
        sums_in.append(b1_sum.reshape(PIECES, 1, step))
    output, grad_two, gain_three, shift_three = acc
    grad_fc_in = summed(jnp.concatenate(grads_in, 2).reshape(D, ff) * factor)
    grad_fc_out = summed(jnp.concatenate(grads_out, 1).reshape(ff, D) * factor)
    sum_fc = jnp.concatenate(sums_in, 1).reshape(-1)

    grad_one, grad_enc, *rest_two = attend_backward(
        scalars,
        grad_two,
        x_one,
        (enc_t,),
        (gains[1], part(vec_two, 0)),
        saved_two,
        first_two,
        second_two,
    )
    grad_hidden, *rest_one = attend_backward(
        scalars,
        grad_one,
        hidden,
        masks,
        (gains[0], part(vec_one, 0)),
        saved_one,
        first_one,
        second_one,
    )

    def attention_grads(rest):
        keep_a, send_a, keep_b, send_b, q_sum, v_sum, b_sum, gain_sum, shift_sum = rest
        grad_a = join_pieces(keep_a, send_a).reshape(D, 2 * D)
        grad_b = join_pieces(keep_b, send_b).reshape(D, 2 * D)
        qkv = jnp.concatenate([grad_a, grad_b[:, :D]], 1)
        vector = jnp.concatenate([shift_sum, q_sum, v_sum, b_sum], 1)[0]
        return (
            summed(qkv * factor),
            summed(grad_b[:, D:] * factor),
            summed(vector * factor),
            gain_sum,
        )

    grad_cross_qkv, grad_cross_out, grad_cross_vec, gain_two = attention_grads(rest_two)
    grad_self_qkv, grad_self_out, grad_self_vec, gain_one = attention_grads(rest_one)
    vector = jnp.concatenate([shift_three[0], jnp.sum(grad_out.astype(F32), 0), sum_fc])
    grad_mlp_vec = summed(vector * factor)
    stacked = jnp.concatenate([gain_one, gain_two, gain_three], 0) * factor
    grad_gain = lax.psum(
        lax.psum_scatter(stacked.astype(BF16), "shard", scatter_dimension=1, tiled=True), "rep"
    ).astype(F32)
    return (
        output,
        grad_hidden,
        grad_enc.reshape(1, ROWS, D),
        grad_gain,
        grad_self_qkv,
        grad_self_out,
        grad_self_vec,
        grad_cross_qkv,
        grad_cross_out,
        grad_cross_vec,
        grad_fc_in,
        grad_fc_out,
        grad_mlp_vec,
    )


def solution(mesh):
    placed = (
        P(("rep", "shard"), None),
        P(("rep", "shard")),
        P(("rep", "shard")),
        P(("rep", "shard"), None, None),
        P(("rep", "shard")),
        P(("rep", "shard"), None),
        P(None, "shard"),
        P("shard", None),
        P("shard", None),
        P("shard"),
        P("shard", None),
        P("shard", None),
        P("shard"),
        P("shard", None),
        P("shard", None),
        P("shard"),
    )
    return jax.shard_map(
        per_device,
        mesh=mesh,
        in_specs=placed,
        out_specs=(
            P(("rep", "shard"), None),
            P(("rep", "shard"), None),
            P(("rep", "shard"), None, None),
            P(None, "shard"),
            P("shard", None),
            P("shard", None),
            P("shard"),
            P("shard", None),
            P("shard", None),
            P("shard"),
            P("shard", None),
            P("shard", None),
            P("shard"),
        ),
        check_vma=False,
    )
```

```python
import functools
import math

import jax
import jax.numpy as jnp
from jax import lax
from jax.experimental import pallas as pl
from jax.experimental.pallas import tpu as pltpu
from jax.sharding import PartitionSpec as P

HEADS = 16
HEAD_DIM = 64
EPSILON = 1e-05
MASKED = -1e30
GELU_A = math.sqrt(2.0 / math.pi)
GELU_B = GELU_A * 0.044715

D = 1024
ROWS = 1024
GROUP = 256
GROUPS = 4
PIECES = 8
QBLOCK = 512
KBLOCK = 256
TILE = 1024
F32 = jnp.float32
BF16 = jnp.bfloat16
VMEM_LIMIT = 62 * 1024 * 1024


def dot(left, right):
    return jnp.dot(left, right, preferred_element_type=F32)


def dot_t(left, right):
    return lax.dot_general(left, right, (((1,), (1,)), ((), ())), preferred_element_type=F32)


def dot_a(left, right):
    return lax.dot_general(left, right, (((0,), (0,)), ((), ())), preferred_element_type=F32)


def normalize(values):
    center = jnp.mean(values, -1, keepdims=True)
    offset = values - center
    scale_inv = lax.rsqrt(jnp.mean(offset * offset, -1, keepdims=True) + EPSILON)
    return offset * scale_inv, scale_inv


def norm_back(grad, values, gain):
    normed, scale_inv = normalize(values)
    scaled = grad * gain
    back = scale_inv * (
        scaled
        - jnp.mean(scaled, -1, keepdims=True)
        - normed * jnp.mean(scaled * normed, -1, keepdims=True)
    )
    return back, jnp.sum(grad * normed, 0, keepdims=True), jnp.sum(grad, 0, keepdims=True)


def split_three(values):
    high = values.astype(BF16)
    rest = values - high.astype(F32)
    middle = rest.astype(BF16)
    return high, middle, (rest - middle.astype(F32)).astype(BF16)


def place(me, rank):
    return lax.bitwise_xor(me, rank)


WHOLE = ((None, 0, 4 * D),)


def shard_rows(me, rank, rows_each):
    if rank is None:
        return pl.ds(0, rows_each * PIECES)
    return pl.ds(pl.multiple_of(place(me, rank) * rows_each, rows_each), rows_each)


def qkv_copies(me, group, layout, parts, weights, sems):
    copies = []
    slot = group % 2
    for number, ((rank, first, count), part_ref) in enumerate(zip(layout, parts)):
        rows = shard_rows(me, rank, D // PIECES)
        for index in range(3):
            if first <= index * D < first + count:
                start = index * D - first + group * GROUP
                source = pl.ds(pl.multiple_of(start, GROUP), GROUP)
                copies.append(
                    pltpu.make_async_copy(
                        part_ref.at[:, source],
                        weights.at[slot, rows, pl.ds(index * GROUP, GROUP)],
                        sems.at[slot, number * 3 + index],
                    )
                )
    return copies


def out_copies(me, layout, parts, out_weights, sems):
    copies = []
    for number, ((rank, first, count), part_ref) in enumerate(zip(layout, parts)):
        if first <= 3 * D < first + count:
            rows = shard_rows(me, rank, D // PIECES)
            source = pl.ds(3 * D - first, D)
            copies.append(
                pltpu.make_async_copy(
                    part_ref.at[:, source], out_weights.at[rows, :], sems.at[number]
                )
            )
    return copies


def start_all(copies):
    for copy in copies:
        copy.start()


def wait_all(copies):
    for copy in copies:
        copy.wait()


def build_self_bias(seg_col, seg_row, pad_row, bias):
    for first in range(0, ROWS, QBLOCK):
        count = first + QBLOCK
        rows = first + lax.broadcasted_iota(jnp.int32, (QBLOCK, count), 0)
        cols = lax.broadcasted_iota(jnp.int32, (QBLOCK, count), 1)
        same = seg_col[first : first + QBLOCK, :] == seg_row[:, :count]
        real = (pad_row[:, :count] == 1) | (cols == rows)
        allowed = (cols <= rows) & same & real
        bias[first : first + QBLOCK, :count] = jnp.where(allowed, 0.0, MASKED)


def lanes_of(half):
    lane = lax.broadcasted_iota(jnp.int32, (1, 128), 1)
    mine = (lane < 64) if half == 0 else (lane >= 64)
    return lane, mine, (64 if half == 0 else 0)


def key_mask(shape, length):
    rows = lax.broadcasted_iota(jnp.int32, shape, 0)
    return jnp.where(rows < length, 0.0, MASKED).astype(BF16)


def forward_pair(query, key, value, length, bias, out_ref, log_ref, pair, causal):
    lane, _, _ = lanes_of(0)
    columns = slice(pair * 128, pair * 128 + 128)
    logs = [[], []]
    for first in range(0, ROWS, QBLOCK):
        count = first + QBLOCK if causal else key.shape[0]
        outs = []
        for half in range(2):
            _, mine, extra = lanes_of(half)
            q_block = query[first : first + QBLOCK]
            if causal:
                q_ext = jnp.where(mine, q_block, jnp.zeros_like(q_block))
                scores = dot_t(q_ext, key[:count]) + bias[first : first + QBLOCK, :count]
            else:
                q_ext = jnp.where(mine, q_block, (lane == extra).astype(BF16))
                k_ext = jnp.where(lane == extra, key_mask(key.shape, length), key)
                scores = dot_t(q_ext, k_ext)
            row_max = jnp.max(scores, 1, keepdims=True)
            weights = jnp.exp(scores - row_max).astype(BF16)
            v_ext = jnp.where(mine, value[:count], jnp.ones_like(value[:count]))
            mixed = dot(weights, v_ext)
            total = mixed[:, extra : extra + 1]
            outs.append((mixed, total))
            log_ref[0, first : first + QBLOCK, 2 * pair + half : 2 * pair + half + 1] = (
                row_max + jnp.log(total)
            )
        numerator = jnp.where(lane < 64, outs[0][0], outs[1][0])
        denominator = jnp.where(lane < 64, outs[0][1], outs[1][1])
        out_ref[first : first + QBLOCK, columns] = (numerator / denominator).astype(BF16)


def attend_forward_body(cross, layout, *refs):
    it = iter(refs)
    scalars = next(it)
    x_ref, a_ref, side = next(it), next(it), next(it)
    out_bias, q_bias, v_bias, gain, shift = (next(it) for _ in range(5))
    parts = [next(it) for _ in layout]
    x_out, next_a, next_t, q_ref, k_ref, v_ref, o_ref, log_ref = (next(it) for _ in range(8))
    weights, out_weights, sems, out_sems = (next(it) for _ in range(4))
    group = pl.program_id(0)
    me = scalars[0]
    length = scalars[1]

    @pl.when(group == 0)
    def _():
        start_all(qkv_copies(me, 0, layout, parts, weights, sems))
        start_all(out_copies(me, layout, parts, out_weights, out_sems))
        x_out[...] = x_ref[...].astype(F32) + out_bias[...]

    @pl.when(group < GROUPS - 1)
    def _():
        start_all(qkv_copies(me, group + 1, layout, parts, weights, sems))

    wait_all(qkv_copies(me, group, layout, parts, weights, sems))

    def block(index):
        return weights[group % 2, :, index * GROUP : (index + 1) * GROUP]

    kv_rows = side[...] if cross else a_ref[...]
    q_ref[...] = ((dot(a_ref[...], block(0)) + q_bias[...]) * 0.125).astype(BF16)
    k_ref[...] = dot(kv_rows, block(1)).astype(BF16)
    v_ref[...] = (dot(kv_rows, block(2)) + v_bias[...]).astype(BF16)
    for pair in range(2):
        columns = slice(pair * 128, pair * 128 + 128)
        forward_pair(
            q_ref[:, columns],
            k_ref[:, columns],
            v_ref[:, columns],
            length,
            side,
            o_ref,
            log_ref,
            pair,
            not cross,
        )

    @pl.when(group == 0)
    def _():
        wait_all(out_copies(me, layout, parts, out_weights, out_sems))

    rows = pl.ds(pl.multiple_of(group * GROUP, GROUP), GROUP)
    x_out[...] += dot(o_ref[...], out_weights[rows, :])

    @pl.when(group == GROUPS - 1)
    def _():
        normed, _ = normalize(x_out[...])
        values = (normed * gain[...] + shift[...]).astype(BF16)
        next_a[...] = values
        next_t[...] = values.T


def whole(shape):
    zeros = (0,) * len(shape)
    return pl.BlockSpec(shape, lambda *_: zeros, pipeline_mode=pl.Buffered(1))


def group_block(rows=ROWS):
    return pl.BlockSpec((rows, GROUP), lambda g, s: (0, g))


ANY = pl.BlockSpec(memory_space=pl.ANY)
PARAMS = pltpu.CompilerParams(vmem_limit_bytes=VMEM_LIMIT)


def shaped(shape, dtype=BF16):
    return jax.ShapeDtypeStruct(shape, dtype)


def skipping(body, leading, count):
    def run(*refs):
        body(*refs[:leading], *refs[leading + count :])

    return run


def cost(flops, nbytes, exps=0):
    return pl.CostEstimate(flops=int(flops), bytes_accessed=int(nbytes), transcendentals=int(exps))


def attend_forward(scalars, x, a, side, vectors, held, deps=()):
    cross = side.dtype == BF16
    layout, parts = held
    return pl.pallas_call(
        skipping(functools.partial(attend_forward_body, cross, layout), 1, len(deps)),
        grid_spec=pltpu.PrefetchScalarGridSpec(
            num_scalar_prefetch=1,
            grid=(GROUPS,),
            in_specs=[ANY] * len(deps)
            + [whole((ROWS, D))] * 3
            + [whole((1, D))]
            + [group_block(1)] * 2
            + [whole((1, D))] * 2
            + [ANY] * len(parts),
            out_specs=[whole((ROWS, D))] * 3
            + [group_block()] * 4
            + [pl.BlockSpec((1, ROWS, 4), lambda g, s: (g, 0, 0))],
            scratch_shapes=[
                pltpu.VMEM((2, D, 3 * GROUP), BF16),
                pltpu.VMEM((D, D), BF16),
                pltpu.SemaphoreType.DMA((2, 3 * len(parts))),
                pltpu.SemaphoreType.DMA((len(parts),)),
            ],
        ),
        out_shape=[shaped((ROWS, D), F32), shaped((ROWS, D)), shaped((D, ROWS))]
        + [shaped((ROWS, D))] * 4
        + [shaped((GROUPS, ROWS, 4), F32)],
        compiler_params=PARAMS,
        cost_estimate=cost(2 * ROWS * D * D * (4 + 8), 30e6, HEADS * ROWS * ROWS),
        name="cross_forward" if cross else "self_forward",
    )(scalars, *deps, x, a, side, *vectors, *parts)


def backward_pair(refs, go_ref, length, bias, accs, pair, causal):
    q_ref, k_ref, v_ref, o_ref, log_ref = refs
    grads, dk_acc, dv_acc = accs
    columns = slice(pair * 128, pair * 128 + 128)
    query, key, value = q_ref[:, columns], k_ref[:, columns], v_ref[:, columns]
    go = go_ref[:, columns]
    q_turned, go_turned = query.T, go.T
    product = go.astype(F32) * o_ref[:, columns].astype(F32)
    zeros = jnp.zeros_like(query)
    q_ext, go_ext, k_ext, v_ext, k_own = [], [], [], [], []
    for half in range(2):
        lane, mine, extra = lanes_of(half)
        delta = jnp.sum(jnp.where(mine, product, 0.0), 1, keepdims=True)
        logs = log_ref[0, :, 2 * pair + half : 2 * pair + half + 1]
        k_own.append(jnp.where(mine, key, zeros))

        def with_rows(base, column, last):
            high, middle, low = split_three(-column)
            filled = jnp.where(lane == extra, high, jnp.where(lane == extra + 1, middle, zeros))
            filled = jnp.where(lane == extra + 2, low, filled)
            filled = jnp.where(lane == extra + 3, last, filled)
            return jnp.where(mine, base, filled)

        ones = ((lane >= extra) & (lane < extra + 3)).astype(BF16)
        one = jnp.ones_like(query)
        q_ext.append(with_rows(query, logs, zeros if causal else one))
        go_ext.append(with_rows(go, delta, zeros))
        keys = jnp.where(mine, key, ones)
        if not causal:
            keys = jnp.where(lane == extra + 3, key_mask(key.shape, length), keys)
        k_ext.append(keys)
        v_ext.append(jnp.where(mine, value, ones))
    last_first = ROWS - KBLOCK
    for first in range(last_first, -1, -KBLOCK):
        rows = slice(first, first + KBLOCK)
        count = first + KBLOCK if causal else key.shape[0]
        grads_q = []
        for half in range(2):
            scores = dot_t(q_ext[half][rows], k_ext[half][:count])
            if causal:
                scores = scores + bias[rows, :count]
            weights = jnp.exp(scores)
            grad_weights = dot_t(go_ext[half][rows], v_ext[half][:count])
            grad_scores = (weights * grad_weights).astype(BF16)
            grads_q.append(dot(grad_scores, k_own[half][:count]))
            dims = slice(64 * half, 64 * half + 64)
            grad_value = dot(go_turned[dims, rows], weights.astype(BF16))
            grad_key = dot(q_turned[dims, rows], grad_scores)
            if first == last_first:
                dv_acc[dims, :] = grad_value
                dk_acc[dims, :] = grad_key
            else:
                dv_acc[dims, :count] += grad_value
                dk_acc[dims, :count] += grad_key
        grads[rows, columns] = (grads_q[0] + grads_q[1]).astype(BF16) * 0.125
    for index, total in ((1, dk_acc), (2, dv_acc)):
        first = index * GROUP + pair * 128
        grads[:, first : first + 128] = total[...].astype(BF16).T


HALF = PIECES // 2


def scatter_rows(me, base, holder, targets, columns):
    shards = holder.shape[0]
    if len(targets) == 1:
        for index in range(shards):
            targets[0][base + index, :, columns] = holder[index]
        return
    keep, send = targets
    for index in range(shards // 2):
        if shards == PIECES:
            slot, pair = index, place(index, me // 2) * 2
        else:
            slot, pair = place(base // 2 + index, me // 2), 2 * index
        keep[slot, :, columns] = holder[pair + me % 2]
        send[slot, :, columns] = holder[pair + (1 - me % 2)]


def attend_backward_body(cross, with_out, natural, *refs):
    it = iter(refs)
    scalars = next(it)
    a_hbm = next(it)
    enc_hbm = next(it) if cross else None
    bias = None if cross else next(it)
    gb, o_rows = (next(it), next(it)) if with_out else (None, None)
    go, q_ref, k_ref, v_ref, o_ref, log_ref = (next(it) for _ in range(6))
    grads = next(it)
    targets = [next(it)] if natural else [next(it), next(it)]
    q_sum, v_sum = next(it), next(it)
    a_t, dk_acc, dv_acc, holder, sem = (next(it) for _ in range(5))
    enc_t = next(it) if cross else None
    holder_out = next(it) if with_out else None
    step = pl.program_id(0)
    me = scalars[0]
    wide = 3 * GROUP

    def loads():
        copies = [pltpu.make_async_copy(a_hbm, a_t, sem.at[0])]
        if cross:
            copies.append(pltpu.make_async_copy(enc_hbm, enc_t, sem.at[1]))
        return copies

    @pl.when(step == 0)
    def _():
        start_all(loads())

    if with_out:
        shards = o_rows.shape[1] // 128
        holder_out[...] = dot(o_rows[...].T, gb[...]).astype(BF16).reshape(shards, 128, D)
        first = targets[0].shape[2] - D
        scatter_rows(me, step * shards, holder_out, targets, slice(first, first + D))
    for pair in range(2):
        backward_pair(
            (q_ref, k_ref, v_ref, o_ref, log_ref),
            go,
            scalars[1],
            bias,
            (grads, dk_acc, dv_acc),
            pair,
            not cross,
        )

    @pl.when(step == 0)
    def _():
        wait_all(loads())

    if cross:
        left = dot(a_t[...], grads[:, :GROUP]).astype(BF16)
        right = dot(enc_t[...], grads[:, GROUP:]).astype(BF16)
        holder[:, :, :GROUP] = left.reshape(PIECES, 128, GROUP)
        holder[:, :, GROUP:] = right.reshape(PIECES, 128, 2 * GROUP)
    else:
        holder[...] = dot(a_t[...], grads[...]).astype(BF16).reshape(PIECES, 128, wide)
    columns = pl.ds(pl.multiple_of(step * wide, GROUP), wide)
    scatter_rows(me, 0, holder, targets, columns)
    q_sum[...] = jnp.sum(grads[:, :GROUP].astype(F32), 0, keepdims=True)
    v_sum[...] = jnp.sum(grads[:, 2 * GROUP :].astype(F32), 0, keepdims=True)


def attend_backward(scalars, base, steps, a_t, side, go, saved, gb, natural, deps=()):
    cross = side.dtype == BF16
    wide = 3 * GROUP
    with_out = gb is not None
    total = steps * wide + (D if with_out else 0)

    def block():
        return pl.BlockSpec((ROWS, GROUP), lambda i, s: (0, base + i))

    scratch = [
        pltpu.VMEM((D, ROWS), BF16),
        pltpu.VMEM((128, ROWS), F32),
        pltpu.VMEM((128, ROWS), F32),
        pltpu.VMEM((PIECES, 128, wide), BF16),
        pltpu.SemaphoreType.DMA((2,)),
    ]
    operands = [a_t, side]
    in_specs = [ANY, ANY if cross else whole((ROWS, ROWS))]
    if cross:
        scratch.append(pltpu.VMEM((D, ROWS), BF16))
    if with_out:
        out_rows = D // steps
        operands += [gb, saved[3]]
        in_specs += [whole((ROWS, D)), pl.BlockSpec((ROWS, out_rows), lambda i, s: (0, i))]
        scratch.append(pltpu.VMEM((out_rows // 128, 128, D), BF16))
    targets = [(PIECES, 128, total)] if natural else [(HALF, 128, total)] * 2
    return pl.pallas_call(
        skipping(functools.partial(attend_backward_body, cross, with_out, natural), 1, len(deps)),
        grid_spec=pltpu.PrefetchScalarGridSpec(
            num_scalar_prefetch=1,
            grid=(steps,),
            in_specs=[ANY] * len(deps)
            + in_specs
            + [block()] * 5
            + [pl.BlockSpec((1, ROWS, 4), lambda i, s: (base + i, 0, 0))],
            out_specs=[pl.BlockSpec((ROWS, wide), lambda i, s: (0, i))]
            + [whole(shape) for shape in targets]
            + [pl.BlockSpec((1, GROUP), lambda i, s: (0, i))] * 2,
            scratch_shapes=scratch,
        ),
        out_shape=[shaped((ROWS, steps * wide))]
        + [shaped(shape) for shape in targets]
        + [shaped((1, steps * GROUP), F32)] * 2,
        compiler_params=PARAMS,
        cost_estimate=cost(2 * ROWS * D * D * (1 + 5 * steps), 20e6, 4 * steps * ROWS * ROWS),
        name="cross_backward" if cross else "self_backward",
    )(scalars, *deps, *operands, go, *saved)


def project_back_body(layout, below_layout, counts, *refs):
    cross = below_layout is not None
    it = iter(refs)
    scalars = next(it)
    grads = [next(it) for _ in counts]
    gx, x_ref, gain = next(it), next(it), next(it)
    parts = [next(it) for _ in layout]
    if cross:
        below = [next(it) for _ in below_layout]
    gx_out, gain_sum, shift_sum = (next(it) for _ in range(3))
    if cross:
        genc, b_sum, gb_out, go = (next(it) for _ in range(4))
    da, weights, sems = (next(it) for _ in range(3))
    if cross:
        denc, out_weights, out_sems = (next(it) for _ in range(3))
    group = pl.program_id(0)
    me = scalars[0]

    @pl.when(group == 0)
    def _():
        start_all(qkv_copies(me, 0, layout, parts, weights, sems))
        if cross:
            start_all(out_copies(me, below_layout, below, out_weights, out_sems))

    @pl.when(group < GROUPS - 1)
    def _():
        start_all(qkv_copies(me, group + 1, layout, parts, weights, sems))

    wait_all(qkv_copies(me, group, layout, parts, weights, sems))

    def go_on(grad, opening):
        tile = weights[group % 2]
        if cross:
            from_q = dot_t(grad[:, :GROUP], tile[:, :GROUP])
            from_kv = dot_t(grad[:, GROUP:], tile[:, GROUP:])
            denc[...] = from_kv if opening else denc[...] + from_kv
        else:
            from_q = dot_t(grad[...], tile)
        da[...] = from_q if opening else da[...] + from_q

    @pl.when(group == 0)
    def _():
        go_on(grads[0], True)

    first = 0
    for grad, count in zip(grads, counts):

        @pl.when((group >= max(first, 1)) & (group < first + count))
        def _(grad=grad):
            go_on(grad, False)

        first += count

    @pl.when(group == GROUPS - 1)
    def _():
        back, gain_grad, shift_grad = norm_back(da[...], x_ref[...].astype(F32), gain[...])
        gain_sum[...] = gain_grad
        shift_sum[...] = shift_grad
        total = gx[...] + back
        gx_out[...] = total.astype(gx_out.dtype)
        if cross:
            genc[...] = denc[...].astype(BF16)
            gb = total.astype(BF16)
            gb_out[...] = gb
            b_sum[...] = jnp.sum(gb.astype(F32), 0, keepdims=True)
            wait_all(out_copies(me, below_layout, below, out_weights, out_sems))
            go[...] = dot_t(gb, out_weights[...]).astype(BF16)


def project_back(scalars, grads, gx, x, gain, held, below=None, deps=()):
    cross = below is not None
    wide = 3 * GROUP
    layout, parts = held
    counts = [grad.shape[1] // wide for grad in grads]
    starts = [sum(counts[:i]) for i in range(len(counts))]

    def grad_spec(start, count):
        return pl.BlockSpec((ROWS, wide), lambda g, s: (0, jnp.clip(g - start, 0, count - 1)))

    operands = [*grads, gx, x, gain, *parts]
    in_specs = [grad_spec(start, count) for start, count in zip(starts, counts)]
    in_specs += [whole((ROWS, D)), whole((ROWS, D)), whole((1, D))] + [ANY] * len(parts)
    out_shape = [shaped((ROWS, D), F32 if cross else BF16)] + [shaped((1, D), F32)] * 2
    scratch = [
        pltpu.VMEM((ROWS, D), F32),
        pltpu.VMEM((2, D, wide), BF16),
        pltpu.SemaphoreType.DMA((2, 3 * len(parts))),
    ]
    if cross:
        operands += [*below[1]]
        in_specs += [ANY] * len(below[1])
        out_shape += [shaped((ROWS, D)), shaped((1, D), F32)] + [shaped((ROWS, D))] * 2
        scratch += [
            pltpu.VMEM((ROWS, D), F32),
            pltpu.VMEM((D, D), BF16),
            pltpu.SemaphoreType.DMA((len(below[1]),)),
        ]
    return pl.pallas_call(
        skipping(
            functools.partial(
                project_back_body, layout, below[0] if cross else None, tuple(counts)
            ),
            1,
            len(deps),
        ),
        grid_spec=pltpu.PrefetchScalarGridSpec(
            num_scalar_prefetch=1,
            grid=(GROUPS,),
            in_specs=[ANY] * len(deps) + in_specs,
            out_specs=[whole(out.shape) for out in out_shape],
            scratch_shapes=scratch,
        ),
        out_shape=out_shape,
        compiler_params=PARAMS,
        cost_estimate=cost(2 * ROWS * D * D * (4 if cross else 3), 30e6),
        name="cross_project" if cross else "self_project",
    )(scalars, *deps, *operands)


def mlp_up_body(a_ref, go, w1, b1, active_out, slope_out, grad_w2):
    unit = dot(a_ref[...], w1[...]) + b1[...]
    square = unit * unit
    gate = 0.5 + 0.5 * jnp.tanh(unit * (GELU_A + GELU_B * square))
    value = unit * gate
    active = value.astype(BF16)
    active_out[...] = active
    slope = gate + value * (1.0 - gate) * (2.0 * GELU_A + 6.0 * GELU_B * square)
    slope_out[...] = slope.astype(BF16)
    grad_w2[...] = dot_a(active, go[...]).astype(BF16)


def mlp_up(a, go, w1, b1, deps=()):
    ff = w1.shape[1]

    def fixed(shape):
        return pl.BlockSpec(shape, lambda i: (0, 0), pipeline_mode=pl.Buffered(1))

    tall = pl.BlockSpec((ROWS, TILE), lambda i: (0, i))
    return pl.pallas_call(
        skipping(mlp_up_body, 0, len(deps)),
        grid=(ff // TILE,),
        in_specs=[ANY] * len(deps)
        + [
            fixed((ROWS, D)),
            fixed((ROWS, D)),
            pl.BlockSpec((D, TILE), lambda i: (0, i)),
            pl.BlockSpec((1, TILE), lambda i: (0, i)),
        ],
        out_specs=[tall, tall, pl.BlockSpec((TILE, D), lambda i: (i, 0))],
        out_shape=[shaped((ROWS, ff)), shaped((ROWS, ff)), shaped((ff, D))],
        compiler_params=PARAMS,
        cost_estimate=cost(2 * 2 * ROWS * D * ff, 60e6, ROWS * ff),
        name="mlp_up",
    )(*deps, a, go, w1, b1)


def row_tile_copies(layout, parts, step, slot, weights, sems, act):
    for number, ((rank, first, count), part_ref) in enumerate(zip(layout, parts)):
        if rank is None:
            rows = pl.ds(pl.multiple_of(step * TILE, TILE), TILE)
            act(pltpu.make_async_copy(part_ref.at[rows, :], weights.at[slot], sems.at[slot]))
            continue
        low = (rank * D + first) // TILE

        @pl.when((step >= low) & (step < low + count // TILE))
        def _(part_ref=part_ref, low=low):
            rows = pl.ds(pl.multiple_of((step - low) * TILE, TILE), TILE)
            act(pltpu.make_async_copy(part_ref.at[rows, :], weights.at[slot], sems.at[slot]))


def tile_of(step, scalars, layout):
    if layout[0][0] is None:
        return step
    per_shard = D // TILE
    return place(scalars[0], step // per_shard) * per_shard + step % per_shard


def start_copy(copy):
    copy.start()


def wait_copy(copy):
    copy.wait()


def mlp_down_body(layout, below_layout, steps, *refs):
    it = iter(refs)
    scalars = next(it)
    a_t, go, slope, w1 = (next(it) for _ in range(4))
    x_hbm, gain = next(it), next(it)
    parts = [next(it) for _ in layout]
    below = [next(it) for _ in below_layout]
    grad_w1, b1_sum, gx_out, gb_out, ga, gain_sum, shift_sum, b_sum = (next(it) for _ in range(8))
    da, w2, sems, x_ref, out_weights, out_sems, sem = (next(it) for _ in range(7))
    step = pl.program_id(0)
    me = scalars[0]
    slot = step % 2

    @pl.when(step == 0)
    def _():
        row_tile_copies(layout, parts, 0, 0, w2, sems, start_copy)
        da[...] = jnp.zeros_like(da)

    @pl.when(step == 1)
    def _():
        start_all(out_copies(me, below_layout, below, out_weights, out_sems))
        pltpu.make_async_copy(x_hbm, x_ref, sem.at[0]).start()

    @pl.when(step < steps - 1)
    def _():
        row_tile_copies(layout, parts, step + 1, 1 - slot, w2, sems, start_copy)

    row_tile_copies(((None, 0, 0),), [parts[0]], 0, slot, w2, sems, wait_copy)
    grad_unit = (dot_t(go[...], w2[slot]) * slope[...].astype(F32)).astype(BF16)
    b1_sum[...] = jnp.sum(grad_unit.astype(F32), 0, keepdims=True)
    grad_w1[...] = dot(a_t[...], grad_unit).astype(BF16)
    da[...] += dot_t(grad_unit, w1[...])

    @pl.when(step == steps - 1)
    def _():
        pltpu.make_async_copy(x_hbm, x_ref, sem.at[0]).wait()
        back, gain_grad, shift_grad = norm_back(da[...], x_ref[...], gain[...])
        gain_sum[...] = gain_grad
        shift_sum[...] = shift_grad
        total = go[...].astype(F32) + back
        gx_out[...] = total
        gb = total.astype(BF16)
        gb_out[...] = gb
        b_sum[...] = jnp.sum(gb.astype(F32), 0, keepdims=True)
        wait_all(out_copies(me, below_layout, below, out_weights, out_sems))
        ga[...] = dot_t(gb, out_weights[...]).astype(BF16)


def mlp_down(scalars, a_t, go, slope, w1, x, gain, held, below, deps=()):
    ff = w1.shape[1]
    steps = ff // TILE
    layout, parts = held
    tall = pl.BlockSpec((ROWS, TILE), lambda i, s: (0, tile_of(i, s, layout)))
    out_shape = [shaped((D, ff)), shaped((1, ff), F32), shaped((ROWS, D), F32)]
    out_shape += [shaped((ROWS, D))] * 2 + [shaped((1, D), F32)] * 3
    return pl.pallas_call(
        skipping(functools.partial(mlp_down_body, layout, below[0], steps), 1, len(deps)),
        grid_spec=pltpu.PrefetchScalarGridSpec(
            num_scalar_prefetch=1,
            grid=(steps,),
            in_specs=[ANY] * len(deps)
            + [whole((D, ROWS)), whole((ROWS, D)), tall, tall, ANY, whole((1, D))]
            + [ANY] * (len(parts) + len(below[1])),
            out_specs=[tall, pl.BlockSpec((1, TILE), lambda i, s: (0, tile_of(i, s, layout)))]
            + [whole(out.shape) for out in out_shape[2:]],
            scratch_shapes=[
                pltpu.VMEM((ROWS, D), F32),
                pltpu.VMEM((2, TILE, D), BF16),
                pltpu.SemaphoreType.DMA((2,)),
                pltpu.VMEM((ROWS, D), F32),
                pltpu.VMEM((D, D), BF16),
                pltpu.SemaphoreType.DMA((len(below[1]),)),
                pltpu.SemaphoreType.DMA((1,)),
            ],
        ),
        out_shape=out_shape,
        compiler_params=PARAMS,
        cost_estimate=cost(3 * 2 * ROWS * D * ff, 60e6),
        name="mlp_down",
    )(scalars, *deps, a_t, go, slope, w1, x, gain, *parts, *below[1])


def mlp_out_body(layout, steps, *refs):
    it = iter(refs)
    scalars = next(it)
    active, x_hbm, vector = (next(it) for _ in range(3))
    parts = [next(it) for _ in layout]
    result = next(it)
    acc, w2, sems, x_ref, sem = (next(it) for _ in range(5))
    step = pl.program_id(0)
    slot = step % 2

    @pl.when(step == 0)
    def _():
        row_tile_copies(layout, parts, 0, 0, w2, sems, start_copy)
        acc[...] = jnp.zeros_like(acc)

    @pl.when(step == 1)
    def _():
        pltpu.make_async_copy(x_hbm, x_ref, sem.at[0]).start()

    @pl.when(step < steps - 1)
    def _():
        row_tile_copies(layout, parts, step + 1, 1 - slot, w2, sems, start_copy)

    row_tile_copies(((None, 0, 0),), [parts[0]], 0, slot, w2, sems, wait_copy)
    acc[...] += dot(active[...], w2[slot])

    @pl.when(step == steps - 1)
    def _():
        pltpu.make_async_copy(x_hbm, x_ref, sem.at[0]).wait()
        result[...] = (x_ref[...] + acc[...] + vector[...]).astype(BF16)


def mlp_out(scalars, active, x, vector, held, deps=()):
    ff = active.shape[1]
    steps = ff // TILE
    layout, parts = held
    return pl.pallas_call(
        skipping(functools.partial(mlp_out_body, layout, steps), 1, len(deps)),
        grid_spec=pltpu.PrefetchScalarGridSpec(
            num_scalar_prefetch=1,
            grid=(steps,),
            in_specs=[ANY] * len(deps)
            + [
                pl.BlockSpec((ROWS, TILE), lambda i, s: (0, tile_of(i, s, layout))),
                ANY,
                whole((1, D)),
            ]
            + [ANY] * len(parts),
            out_specs=whole((ROWS, D)),
            scratch_shapes=[
                pltpu.VMEM((ROWS, D), F32),
                pltpu.VMEM((2, TILE, D), BF16),
                pltpu.SemaphoreType.DMA((2,)),
                pltpu.VMEM((ROWS, D), F32),
                pltpu.SemaphoreType.DMA((1,)),
            ],
        ),
        out_shape=shaped((ROWS, D)),
        compiler_params=PARAMS,
        cost_estimate=cost(2 * ROWS * D * ff, 40e6),
        name="mlp_out",
    )(scalars, *deps, active, x, vector, *parts)


def prepare_body(x_ref, gain, shift, seg_col, seg_row, pad_row, a_ref, a_t, bias):
    normed, _ = normalize(x_ref[...].astype(F32))
    values = (normed * gain[...] + shift[...]).astype(BF16)
    a_ref[...] = values
    a_t[...] = values.T
    bias[...] = jnp.full_like(bias, MASKED)
    build_self_bias(seg_col, seg_row, pad_row, bias)


def prepare(x, gain, shift, masks):
    return pl.pallas_call(
        prepare_body,
        out_shape=[shaped((ROWS, D)), shaped((D, ROWS)), shaped((ROWS, ROWS), F32)],
        compiler_params=PARAMS,
        name="prepare",
    )(x, gain, shift, *masks)


CORE, XBIT, YBIT = 1, 2, 4


def gather_vectors(ln_gain, self_vec, cross_vec, mlp_vec):
    sizes = [3 * ln_gain.shape[1], self_vec.shape[0], cross_vec.shape[0], mlp_vec.shape[0]]
    packed = jnp.concatenate([ln_gain.reshape(-1), self_vec, cross_vec, mlp_vec])
    every = lax.all_gather(packed, "shard").astype(F32)
    ends = [sum(sizes[: i + 1]) for i in range(4)]
    gains = every[:, : ends[0]].reshape(-1, 3, ln_gain.shape[1]).transpose(1, 0, 2)
    gains = gains.reshape(3, 1, D)
    return [gains] + [every[:, a:b].reshape(1, -1) for a, b in zip(ends[:3], ends[1:])]


def join_heads_body(factor, counts, *refs):
    *sources, target, out = refs
    group = 0
    for source, count in zip(sources, counts):
        for inner in range(count):
            for index in range(3):
                first = index * D + group * GROUP
                start = inner * 3 * GROUP + index * GROUP
                target[:, first : first + GROUP] = (
                    source[:, start : start + GROUP].astype(F32) * factor
                )
            group += 1
        if source.shape[1] > count * 3 * GROUP:
            out[...] = source[:, count * 3 * GROUP :].astype(F32) * factor


def join_heads(parts, factor):
    rows = parts[0].shape[0]
    wide = 3 * GROUP
    counts = [(p.shape[1] - (D if p.shape[1] % wide else 0)) // wide for p in parts]
    return pl.pallas_call(
        functools.partial(join_heads_body, factor, counts),
        out_shape=[shaped((rows, 3 * D), F32), shaped((rows, D), F32)],
        compiler_params=PARAMS,
        name="join_heads",
    )(*parts)


def swap(value, axis, bit):
    size = lax.axis_size(axis)
    return lax.ppermute(value, axis, [(i, i ^ bit) for i in range(size)])


def add(left, right, zero):
    return (left.astype(F32) + (right.astype(F32) + zero)).astype(BF16)


def zero_of(token):
    return token.reshape(-1)[0].astype(F32) * 0.0


def held_back(value, token):
    return value + zero_of(token).astype(value.dtype)


def spread(own, axis):
    (by_x, by_y), zero = yield [(own, "shard", XBIT), (own, "shard", YBIT)]
    zero = zero.astype(own.dtype)
    size = own.shape[axis]
    half = size // 2
    low = lax.slice_in_dim(by_x, 0, half, axis=axis) + zero
    high = lax.slice_in_dim(by_y, half, size, axis=axis) + zero
    far = [(low, "shard", YBIT), (high, "shard", XBIT)]
    far, _ = yield far + [(v, "shard", CORE) for v in (own, by_x, by_y)]
    last, _ = yield [(far[0], "shard", CORE), (far[1], "shard", CORE)]
    layout = [(0, 0, size), (2, 0, size), (4, 0, size), (1, 0, size), (3, 0, size), (5, 0, size)]
    layout += [(6, 0, half), (6, half, half), (7, 0, half), (7, half, half)]
    return tuple(layout), [own, by_x, by_y, *far[2:], *far[:2], *last]


def over_copies(value):
    copies = lax.axis_size("rep")
    if copies == 1:
        return value
    odd = lax.axis_index("rep") % 2 == 1
    rows = value.shape[0] // 2
    low, high = value[:rows], value[rows:]
    (got,), zero = yield [(jnp.where(odd, low, high), "rep", 1)]
    total = add(jnp.where(odd, high, low), got, zero)
    bit = 2
    while bit < copies:
        (got,), zero = yield [(total, "rep", bit)]
        total = add(total, got, zero)
        bit *= 2
    (other,), _ = yield [(total, "rep", 1)]
    return jnp.concatenate([jnp.where(odd, other, total), jnp.where(odd, total, other)], 0)


def reduce(keep, send):
    half = keep.shape[2] // 2
    (got,), zero = yield [(send, "shard", CORE)]
    total = add(keep, got, zero)
    sum_a, sum_b = total[..., :half], total[..., half:]
    got, zero = yield [(sum_a[1::2], "shard", XBIT), (sum_b[2:], "shard", YBIT)]
    half_a, half_b = add(sum_a[0::2], got[0], zero), add(sum_b[:2], got[1], zero)
    got, zero = yield [(half_a[1], "shard", YBIT), (half_b[1], "shard", XBIT)]
    owned = [add(half_a[0], got[0], zero), add(half_b[0], got[1], zero)]
    owned = yield from over_copies(jnp.concatenate(owned, 1))
    return owned


def sum_everywhere(vector):
    for axis in ("shard", "rep"):
        bit = 1
        while bit < lax.axis_size(axis):
            (got,), zero = yield [(vector, axis, bit)]
            vector = vector + (got + zero)
            bit *= 2
    return vector


class Flow:
    def __init__(self):
        self.active = {}
        self.results = {}
        self.deps = []

    def start(self, name, steps):
        self._request(name, steps, next(steps))

    def _request(self, name, steps, wanted):
        self.deps += [array for array, _, _ in wanted]
        self.active[name] = (steps, [swap(*want) for want in wanted])

    def meet(self, token, *names):
        zero = zero_of(token)
        for name in [n for n in names if n in self.active]:
            steps, arrays = self.active[name]
            try:
                self._request(name, steps, steps.send((arrays, zero)))
            except StopIteration as end:
                del self.active[name]
                self.results[name] = end.value

    def take(self):
        deps, self.deps = self.deps, []
        return deps


def part(vector, index):
    return vector[:, index * D : (index + 1) * D]


def forward_vectors(gains, vectors, layer):
    vector, below = vectors[layer], vectors[layer + 1]
    return (
        part(vector, 3),
        part(vector, 1),
        part(vector, 2),
        gains[layer + 1],
        part(below, 0),
    )


def gather(value):
    return lax.all_gather(value, "shard", axis=0, tiled=True)


def scattered(value):
    return lax.psum_scatter(value, "shard", scatter_dimension=0, tiled=True)


def ring_device(
    hidden,
    segments,
    pad_mask,
    encoder,
    src_len,
    grad_out,
    ln_gain,
    self_qkv,
    self_out,
    self_vec,
    cross_qkv,
    cross_out,
    cross_vec,
    fc_in,
    fc_out,
    mlp_vec,
):
    shards = lax.axis_size("shard")
    factor = 1.0 / math.sqrt(ROWS * lax.axis_size("rep") * shards)
    me = lax.axis_index("shard").astype(jnp.int32)
    scalars = jnp.stack([me, src_len[0]])
    flow = Flow()
    ff = fc_in.shape[1]

    gains, *vectors = gather_vectors(ln_gain, self_vec, cross_vec, mlp_vec)
    own_one = held_back(jnp.concatenate([self_qkv, self_out], 1), gains)
    flow.start("self", spread(own_one, 1))
    by_x, by_y = flow.active["self"][1]
    near = zero_of(by_x) + zero_of(by_y)
    encoded = encoder.reshape(ROWS, D)
    enc_t = encoded.T
    masks = (segments.reshape(ROWS, 1), segments.reshape(1, ROWS), pad_mask.reshape(1, ROWS))
    a_one, a_one_t, bias = prepare(hidden, gains[0], part(vectors[0], 0), masks)
    out_sum = jnp.sum(grad_out.astype(F32), 0)
    while "self" in flow.active:
        flow.meet(a_one_t, "self")
    held_one = flow.results["self"]
    all_two = gather(held_back(jnp.concatenate([cross_qkv, cross_out], 1), near))
    all_in, all_out = gather(fc_in), gather(fc_out)
    held_two, held_out = (WHOLE, [all_two]), (WHOLE, [all_out])
    flow.take()
    x_one, a_two, a_two_t, *saved_one = attend_forward(
        scalars, hidden, a_one, bias, forward_vectors(gains, vectors, 0), held_one
    )
    x_two, a_three, a_three_t, *saved_two = attend_forward(
        scalars, x_one, a_two, encoded, forward_vectors(gains, vectors, 1), held_two
    )
    active, slope, grad_w2 = mlp_up(a_three, grad_out, all_in, part_from(vectors[2], 2))
    scattered_out = scattered(grad_w2)
    grad_w1, sum_fc, grad_two, gb_two, ga_two, gain_three, shift_three, out_two = mlp_down(
        scalars, a_three_t, grad_out, slope, all_in, x_two, gains[2], held_out, held_two
    )
    scattered_in = scattered(grad_w1)
    halves_two, *weights_two, q_two, v_two = attend_backward(
        scalars, 0, GROUPS, a_two_t, enc_t, ga_two, saved_two, gb_two, False
    )
    flow.start("cross", reduce(*weights_two))
    flow.start("out", over_copies(held_back(scattered_out, v_two)))
    grad_one, gain_two, shift_two, grad_enc, out_one, gb_one, ga_one = project_back(
        scalars,
        [halves_two],
        grad_two,
        x_one,
        gains[1],
        held_two,
        held_one,
        deps=flow.take(),
    )
    flow.meet(gain_two, "cross", "out")
    early = [gain_three[0], shift_three[0], out_sum, sum_fc[0]]
    early += [gain_two[0], shift_two[0], q_two[0], v_two[0], out_two[0]]
    flow.start("early", sum_everywhere(jnp.concatenate(early)))
    half = GROUPS // 2

    def self_backward(index):
        return attend_backward(
            scalars,
            index * half,
            half,
            a_one_t,
            bias,
            ga_one,
            saved_one,
            gb_one if index == 0 else None,
            False,
            deps=flow.take(),
        )

    grads_low, *weights, q_low, v_low = self_backward(0)
    flow.meet(v_low, "cross", "early")
    flow.start(("self", 0), reduce(*weights))
    grads_high, *weights, q_high, v_high = self_backward(1)
    flow.meet(v_high, "cross", "early", "out", ("self", 0))
    flow.start(("self", 1), reduce(*weights))
    flow.start("in", over_copies(held_back(scattered_in, v_high)))
    output = mlp_out(
        scalars, active, x_two, part(vectors[2], 1), held_out, deps=flow.take()
    )
    flow.meet(output, *flow.active)
    grad_hidden, gain_one, shift_one = project_back(
        scalars, [grads_low, grads_high], grad_one, hidden, gains[0], held_one, deps=flow.take()
    )
    late = [gain_one[0], shift_one[0], q_low[0], q_high[0], v_low[0], v_high[0], out_one[0]]
    flow.start("late", sum_everywhere(jnp.concatenate(late)))
    token = gain_one
    while flow.active:
        flow.take()
        quick = [n for n in flow.active if n != "in"]
        flow.meet(token, *quick)
        deps = flow.take()
        if "in" in flow.active:
            if deps:
                token = sum(zero_of(d) for d in deps)
            flow.meet(token, "in")
            deps += flow.take()
        if deps:
            token = sum(zero_of(d) for d in deps)
    scale = factor
    factor = factor + zero_of(gain_one)
    done = flow.results

    def own(vector):
        size = vector.shape[0] // shards
        return lax.dynamic_slice_in_dim(vector, me * size, size) * factor

    base = 3 * D + ff
    early, late = done["early"], done["late"]
    grad_gain = jnp.stack([own(late[:D]), own(early[base : base + D]), own(early[:D])], 0)
    return (
        output,
        grad_hidden,
        grad_enc.reshape(1, ROWS, D),
        grad_gain,
        *join_heads([done[("self", 0)], done[("self", 1)]], scale),
        own(late[D:]),
        *join_heads([done["cross"]], scale),
        own(early[base + D :]),
        done["in"].astype(F32) * factor,
        done["out"].astype(F32) * factor,
        own(early[D:base]),
    )


def part_from(vector, index):
    return vector[:, index * D :]


def gather_device(
    hidden,
    segments,
    pad_mask,
    encoder,
    src_len,
    grad_out,
    ln_gain,
    self_qkv,
    self_out,
    self_vec,
    cross_qkv,
    cross_out,
    cross_vec,
    fc_in,
    fc_out,
    mlp_vec,
):
    shards = lax.axis_size("shard")
    factor = 1.0 / math.sqrt(ROWS * lax.axis_size("rep") * shards)
    scalars = jnp.stack([jnp.int32(0), src_len[0]])
    encoded = encoder.reshape(ROWS, D)
    enc_t = encoded.T
    gains, *vectors = gather_vectors(ln_gain, self_vec, cross_vec, mlp_vec)
    held_one = (WHOLE, [gather(jnp.concatenate([self_qkv, self_out], 1))])
    held_two = (WHOLE, [gather(jnp.concatenate([cross_qkv, cross_out], 1))])
    all_in, held_out = gather(fc_in), (WHOLE, [gather(fc_out)])
    masks = (segments.reshape(ROWS, 1), segments.reshape(1, ROWS), pad_mask.reshape(1, ROWS))
    a_one, a_one_t, bias = prepare(hidden, gains[0], part(vectors[0], 0), masks)
    x_one, a_two, a_two_t, *saved_one = attend_forward(
        scalars, hidden, a_one, bias, forward_vectors(gains, vectors, 0), held_one
    )
    x_two, a_three, a_three_t, *saved_two = attend_forward(
        scalars, x_one, a_two, encoded, forward_vectors(gains, vectors, 1), held_two
    )
    active, slope, grad_w2 = mlp_up(a_three, grad_out, all_in, part_from(vectors[2], 2))
    grad_w1, sum_fc, grad_two, gb_two, ga_two, gain_three, shift_three, out_two = mlp_down(
        scalars, a_three_t, grad_out, slope, all_in, x_two, gains[2], held_out, held_two
    )
    halves_two, weights_two, q_two, v_two = attend_backward(
        scalars, 0, GROUPS, a_two_t, enc_t, ga_two, saved_two, gb_two, True
    )
    grad_one, gain_two, shift_two, grad_enc, out_one, gb_one, ga_one = project_back(
        scalars, [halves_two], grad_two, x_one, gains[1], held_two, held_one
    )
    halves_one, weights_one, q_one, v_one = attend_backward(
        scalars, 0, GROUPS, a_one_t, bias, ga_one, saved_one, gb_one, True
    )
    grad_hidden, gain_one, shift_one = project_back(
        scalars, [halves_one], grad_one, hidden, gains[0], held_one
    )
    output = mlp_out(scalars, active, x_two, part(vectors[2], 1), held_out)

    def summed(value):
        return lax.psum(scattered(value.astype(BF16)), "rep")

    def final(value):
        return summed(value).astype(F32) * factor

    ones = [shift_one[0], q_one[0], v_one[0], out_one[0]]
    twos = [shift_two[0], q_two[0], v_two[0], out_two[0]]
    threes = [shift_three[0], jnp.sum(grad_out.astype(F32), 0), sum_fc[0]]
    gain = jnp.concatenate([gain_one, gain_two, gain_three], 0)
    return (
        output,
        grad_hidden,
        grad_enc.reshape(1, ROWS, D),
        final(gain.T).T,
        *join_heads([summed(weights_one.reshape(D, -1))], factor),
        final(jnp.concatenate(ones)),
        *join_heads([summed(weights_two.reshape(D, -1))], factor),
        final(jnp.concatenate(twos)),
        final(grad_w1),
        final(grad_w2),
        final(jnp.concatenate(threes)),
    )


def per_device(*arrays):
    copies = lax.axis_size("rep")
    if lax.axis_size("shard") == PIECES and copies & (copies - 1) == 0:
        return ring_device(*arrays)
    return gather_device(*arrays)


def solution(mesh):
    placed = (
        P(("rep", "shard"), None),
        P(("rep", "shard")),
        P(("rep", "shard")),
        P(("rep", "shard"), None, None),
        P(("rep", "shard")),
        P(("rep", "shard"), None),
        P(None, "shard"),
        P("shard", None),
        P("shard", None),
        P("shard"),
        P("shard", None),
        P("shard", None),
        P("shard"),
        P("shard", None),
        P("shard", None),
        P("shard"),
    )
    return jax.shard_map(
        per_device,
        mesh=mesh,
        in_specs=placed,
        out_specs=(
            P(("rep", "shard"), None),
            P(("rep", "shard"), None),
            P(("rep", "shard"), None, None),
            P(None, "shard"),
            P("shard", None),
            P("shard", None),
            P("shard"),
            P("shard", None),
            P("shard", None),
            P("shard"),
            P("shard", None),
            P("shard", None),
            P("shard"),
        ),
        check_vma=False,
    )
```

```python
import functools
import math

import jax
import jax.numpy as jnp
from jax import lax
from jax.experimental import pallas as pl
from jax.experimental.pallas import tpu as pltpu
from jax.sharding import PartitionSpec as P

HEADS = 16
HEAD_DIM = 64
EPSILON = 1e-05
MASKED = -1e30
GELU_A = math.sqrt(2.0 / math.pi)
GELU_B = GELU_A * 0.044715

D = 1024
ROWS = 1024
GROUP = 256
GROUPS = 4
PIECES = 8
QBLOCK = 512
KBLOCK = 256
TILE = 1024
F32 = jnp.float32
BF16 = jnp.bfloat16
VMEM_LIMIT = 62 * 1024 * 1024


def dot(left, right):
    return jnp.dot(left, right, preferred_element_type=F32)


def dot_t(left, right):
    return lax.dot_general(left, right, (((1,), (1,)), ((), ())), preferred_element_type=F32)


def dot_a(left, right):
    return lax.dot_general(left, right, (((0,), (0,)), ((), ())), preferred_element_type=F32)


def normalize(values):
    center = jnp.mean(values, -1, keepdims=True)
    offset = values - center
    scale_inv = lax.rsqrt(jnp.mean(offset * offset, -1, keepdims=True) + EPSILON)
    return offset * scale_inv, scale_inv


def norm_back(grad, values, gain):
    normed, scale_inv = normalize(values)
    scaled = grad * gain
    back = scale_inv * (
        scaled
        - jnp.mean(scaled, -1, keepdims=True)
        - normed * jnp.mean(scaled * normed, -1, keepdims=True)
    )
    return back, jnp.sum(grad * normed, 0, keepdims=True), jnp.sum(grad, 0, keepdims=True)


def split_three(values):
    high = values.astype(BF16)
    rest = values - high.astype(F32)
    middle = rest.astype(BF16)
    return high, middle, (rest - middle.astype(F32)).astype(BF16)


def place(me, rank):
    return lax.bitwise_xor(me, rank)


WHOLE = ((None, 0, 4 * D),)
WHOLE_ROWS = ((None, 0, D),)


def shard_rows(me, rank, rows_each):
    if rank is None:
        return pl.ds(0, rows_each * PIECES)
    return pl.ds(pl.multiple_of(place(me, rank) * rows_each, rows_each), rows_each)


def qkv_copies(me, group, layout, parts, weights, sems):
    copies = []
    slot = group % 2
    for number, ((rank, first, count), part_ref) in enumerate(zip(layout, parts)):
        rows = shard_rows(me, rank, D // PIECES)
        for index in range(3):
            if first <= index * D < first + count:
                start = index * D - first + group * GROUP
                source = pl.ds(pl.multiple_of(start, GROUP), GROUP)
                copies.append(
                    pltpu.make_async_copy(
                        part_ref.at[:, source],
                        weights.at[slot, rows, pl.ds(index * GROUP, GROUP)],
                        sems.at[slot, number * 3 + index],
                    )
                )
    return copies


def out_copies(me, layout, parts, out_weights, sems):
    copies = []
    for number, ((rank, first, count), part_ref) in enumerate(zip(layout, parts)):
        if first <= 3 * D < first + count:
            rows = shard_rows(me, rank, D // PIECES)
            source = pl.ds(3 * D - first, D)
            copies.append(
                pltpu.make_async_copy(
                    part_ref.at[:, source], out_weights.at[rows, :], sems.at[number]
                )
            )
    return copies


def start_all(copies):
    for copy in copies:
        copy.start()


def wait_all(copies):
    for copy in copies:
        copy.wait()


def build_self_bias(seg_col, seg_row, pad_row, bias):
    for first in range(0, ROWS, QBLOCK):
        count = first + QBLOCK
        rows = first + lax.broadcasted_iota(jnp.int32, (QBLOCK, count), 0)
        cols = lax.broadcasted_iota(jnp.int32, (QBLOCK, count), 1)
        same = seg_col[first : first + QBLOCK, :] == seg_row[:, :count]
        real = (pad_row[:, :count] == 1) | (cols == rows)
        allowed = (cols <= rows) & same & real
        bias[first : first + QBLOCK, :count] = jnp.where(allowed, 0.0, MASKED)


def lanes_of(half):
    lane = lax.broadcasted_iota(jnp.int32, (1, 128), 1)
    mine = (lane < 64) if half == 0 else (lane >= 64)
    return lane, mine, (64 if half == 0 else 0)


def key_mask(shape, length):
    rows = lax.broadcasted_iota(jnp.int32, shape, 0)
    return jnp.where(rows < length, 0.0, MASKED).astype(BF16)


def forward_pair(query, key, value, length, bias, out_ref, log_ref, pair, causal):
    lane, _, _ = lanes_of(0)
    columns = slice(pair * 128, pair * 128 + 128)
    logs = [[], []]
    for first in range(0, ROWS, QBLOCK):
        count = first + QBLOCK if causal else key.shape[0]
        outs = []
        for half in range(2):
            _, mine, extra = lanes_of(half)
            q_block = query[first : first + QBLOCK]
            if causal:
                q_ext = jnp.where(mine, q_block, jnp.zeros_like(q_block))
                scores = dot_t(q_ext, key[:count]) + bias[first : first + QBLOCK, :count]
            else:
                q_ext = jnp.where(mine, q_block, (lane == extra).astype(BF16))
                k_ext = jnp.where(lane == extra, key_mask(key.shape, length), key)
                scores = dot_t(q_ext, k_ext)
            row_max = jnp.max(scores, 1, keepdims=True)
            weights = jnp.exp(scores - row_max).astype(BF16)
            v_ext = jnp.where(mine, value[:count], jnp.ones_like(value[:count]))
            mixed = dot(weights, v_ext)
            total = mixed[:, extra : extra + 1]
            outs.append((mixed, total))
            log_ref[0, first : first + QBLOCK, 2 * pair + half : 2 * pair + half + 1] = (
                row_max + jnp.log(total)
            )
        numerator = jnp.where(lane < 64, outs[0][0], outs[1][0])
        denominator = jnp.where(lane < 64, outs[0][1], outs[1][1])
        out_ref[first : first + QBLOCK, columns] = (numerator / denominator).astype(BF16)


def attend_forward_body(cross, layout, *refs):
    it = iter(refs)
    scalars = next(it)
    x_ref, a_ref, side = next(it), next(it), next(it)
    out_bias, q_bias, v_bias, gain, shift = (next(it) for _ in range(5))
    parts = [next(it) for _ in layout]
    x_out, next_a, next_t, q_ref, k_ref, v_ref, o_ref, log_ref = (next(it) for _ in range(8))
    weights, out_weights, sems, out_sems = (next(it) for _ in range(4))
    group = pl.program_id(0)
    me = scalars[0]
    length = scalars[1]

    @pl.when(group == 0)
    def _():
        start_all(qkv_copies(me, 0, layout, parts, weights, sems))
        start_all(out_copies(me, layout, parts, out_weights, out_sems))
        x_out[...] = x_ref[...].astype(F32) + out_bias[...]

    @pl.when(group < GROUPS - 1)
    def _():
        start_all(qkv_copies(me, group + 1, layout, parts, weights, sems))

    wait_all(qkv_copies(me, group, layout, parts, weights, sems))

    def block(index):
        return weights[group % 2, :, index * GROUP : (index + 1) * GROUP]

    kv_rows = side[...] if cross else a_ref[...]
    q_ref[...] = ((dot(a_ref[...], block(0)) + q_bias[...]) * 0.125).astype(BF16)
    k_ref[...] = dot(kv_rows, block(1)).astype(BF16)
    v_ref[...] = (dot(kv_rows, block(2)) + v_bias[...]).astype(BF16)
    for pair in range(2):
        columns = slice(pair * 128, pair * 128 + 128)
        forward_pair(
            q_ref[:, columns],
            k_ref[:, columns],
            v_ref[:, columns],
            length,
            side,
            o_ref,
            log_ref,
            pair,
            not cross,
        )

    @pl.when(group == 0)
    def _():
        wait_all(out_copies(me, layout, parts, out_weights, out_sems))

    rows = pl.ds(pl.multiple_of(group * GROUP, GROUP), GROUP)
    x_out[...] += dot(o_ref[...], out_weights[rows, :])

    @pl.when(group == GROUPS - 1)
    def _():
        normed, _ = normalize(x_out[...])
        values = (normed * gain[...] + shift[...]).astype(BF16)
        next_a[...] = values
        next_t[...] = values.T


def whole(shape):
    zeros = (0,) * len(shape)
    return pl.BlockSpec(shape, lambda *_: zeros, pipeline_mode=pl.Buffered(1))


def group_block(rows=ROWS):
    return pl.BlockSpec((rows, GROUP), lambda g, s: (0, g))


ANY = pl.BlockSpec(memory_space=pl.ANY)
PARAMS = pltpu.CompilerParams(vmem_limit_bytes=VMEM_LIMIT)


def shaped(shape, dtype=BF16):
    return jax.ShapeDtypeStruct(shape, dtype)


def skipping(body, leading, count):
    def run(*refs):
        body(*refs[:leading], *refs[leading + count :])

    return run


def cost(flops, nbytes, exps=0):
    return pl.CostEstimate(flops=int(flops), bytes_accessed=int(nbytes), transcendentals=int(exps))


def attend_forward(scalars, x, a, side, vectors, held, deps=()):
    cross = side.dtype == BF16
    layout, parts = held
    return pl.pallas_call(
        skipping(functools.partial(attend_forward_body, cross, layout), 1, len(deps)),
        grid_spec=pltpu.PrefetchScalarGridSpec(
            num_scalar_prefetch=1,
            grid=(GROUPS,),
            in_specs=[ANY] * len(deps)
            + [whole((ROWS, D))] * 3
            + [whole((1, D))]
            + [group_block(1)] * 2
            + [whole((1, D))] * 2
            + [ANY] * len(parts),
            out_specs=[whole((ROWS, D))] * 3
            + [group_block()] * 4
            + [pl.BlockSpec((1, ROWS, 4), lambda g, s: (g, 0, 0))],
            scratch_shapes=[
                pltpu.VMEM((2, D, 3 * GROUP), BF16),
                pltpu.VMEM((D, D), BF16),
                pltpu.SemaphoreType.DMA((2, 3 * len(parts))),
                pltpu.SemaphoreType.DMA((len(parts),)),
            ],
        ),
        out_shape=[shaped((ROWS, D), F32), shaped((ROWS, D)), shaped((D, ROWS))]
        + [shaped((ROWS, D))] * 4
        + [shaped((GROUPS, ROWS, 4), F32)],
        compiler_params=PARAMS,
        cost_estimate=cost(2 * ROWS * D * D * (4 + 8), 30e6, HEADS * ROWS * ROWS),
        name="cross_forward" if cross else "self_forward",
    )(scalars, *deps, x, a, side, *vectors, *parts)


def backward_pair(refs, go_ref, length, bias, accs, pair, causal):
    q_ref, k_ref, v_ref, o_ref, log_ref = refs
    grads, dk_acc, dv_acc = accs
    columns = slice(pair * 128, pair * 128 + 128)
    query, key, value = q_ref[:, columns], k_ref[:, columns], v_ref[:, columns]
    go = go_ref[:, columns]
    q_turned, go_turned = query.T, go.T
    product = go.astype(F32) * o_ref[:, columns].astype(F32)
    zeros = jnp.zeros_like(query)
    q_ext, go_ext, k_ext, v_ext, k_own = [], [], [], [], []
    for half in range(2):
        lane, mine, extra = lanes_of(half)
        delta = jnp.sum(jnp.where(mine, product, 0.0), 1, keepdims=True)
        logs = log_ref[0, :, 2 * pair + half : 2 * pair + half + 1]
        k_own.append(jnp.where(mine, key, zeros))

        def with_rows(base, column, last):
            high, middle, low = split_three(-column)
            filled = jnp.where(lane == extra, high, jnp.where(lane == extra + 1, middle, zeros))
            filled = jnp.where(lane == extra + 2, low, filled)
            filled = jnp.where(lane == extra + 3, last, filled)
            return jnp.where(mine, base, filled)

        ones = ((lane >= extra) & (lane < extra + 3)).astype(BF16)
        one = jnp.ones_like(query)
        q_ext.append(with_rows(query, logs, zeros if causal else one))
        go_ext.append(with_rows(go, delta, zeros))
        keys = jnp.where(mine, key, ones)
        if not causal:
            keys = jnp.where(lane == extra + 3, key_mask(key.shape, length), keys)
        k_ext.append(keys)
        v_ext.append(jnp.where(mine, value, ones))
    last_first = ROWS - KBLOCK
    for first in range(last_first, -1, -KBLOCK):
        rows = slice(first, first + KBLOCK)
        count = first + KBLOCK if causal else key.shape[0]
        grads_q = []
        for half in range(2):
            scores = dot_t(q_ext[half][rows], k_ext[half][:count])
            if causal:
                scores = scores + bias[rows, :count]
            weights = jnp.exp(scores)
            grad_weights = dot_t(go_ext[half][rows], v_ext[half][:count])
            grad_scores = (weights * grad_weights).astype(BF16)
            grads_q.append(dot(grad_scores, k_own[half][:count]))
            dims = slice(64 * half, 64 * half + 64)
            grad_value = dot(go_turned[dims, rows], weights.astype(BF16))
            grad_key = dot(q_turned[dims, rows], grad_scores)
            if first == last_first:
                dv_acc[dims, :] = grad_value
                dk_acc[dims, :] = grad_key
            else:
                dv_acc[dims, :count] += grad_value
                dk_acc[dims, :count] += grad_key
        grads[rows, columns] = (grads_q[0] + grads_q[1]).astype(BF16) * 0.125
    for index, total in ((1, dk_acc), (2, dv_acc)):
        first = index * GROUP + pair * 128
        grads[:, first : first + 128] = total[...].astype(BF16).T


HALF = PIECES // 2


def scatter_rows(me, base, holder, targets, columns):
    shards = holder.shape[0]
    if len(targets) == 1:
        for index in range(shards):
            targets[0][base + index, :, columns] = holder[index]
        return
    keep, send = targets
    for index in range(shards // 2):
        if shards == PIECES:
            slot, pair = index, place(index, me // 2) * 2
        else:
            slot, pair = place(base // 2 + index, me // 2), 2 * index
        keep[slot, :, columns] = holder[pair + me % 2]
        send[slot, :, columns] = holder[pair + (1 - me % 2)]


def attend_backward_body(cross, with_out, natural, *refs):
    it = iter(refs)
    scalars = next(it)
    a_hbm = next(it)
    enc_hbm = next(it) if cross else None
    bias = None if cross else next(it)
    gb, o_rows = (next(it), next(it)) if with_out else (None, None)
    go, q_ref, k_ref, v_ref, o_ref, log_ref = (next(it) for _ in range(6))
    grads = next(it)
    targets = [next(it)] if natural else [next(it), next(it)]
    q_sum, v_sum = next(it), next(it)
    a_t, dk_acc, dv_acc, holder, sem = (next(it) for _ in range(5))
    enc_t = next(it) if cross else None
    holder_out = next(it) if with_out else None
    step = pl.program_id(0)
    me = scalars[0]
    wide = 3 * GROUP

    def loads():
        copies = [pltpu.make_async_copy(a_hbm, a_t, sem.at[0])]
        if cross:
            copies.append(pltpu.make_async_copy(enc_hbm, enc_t, sem.at[1]))
        return copies

    @pl.when(step == 0)
    def _():
        start_all(loads())

    if with_out:
        shards = o_rows.shape[1] // 128
        holder_out[...] = dot(o_rows[...].T, gb[...]).astype(BF16).reshape(shards, 128, D)
        first = targets[0].shape[2] - D
        scatter_rows(me, step * shards, holder_out, targets, slice(first, first + D))
    for pair in range(2):
        backward_pair(
            (q_ref, k_ref, v_ref, o_ref, log_ref),
            go,
            scalars[1],
            bias,
            (grads, dk_acc, dv_acc),
            pair,
            not cross,
        )

    @pl.when(step == 0)
    def _():
        wait_all(loads())

    if cross:
        left = dot(a_t[...], grads[:, :GROUP]).astype(BF16)
        right = dot(enc_t[...], grads[:, GROUP:]).astype(BF16)
        holder[:, :, :GROUP] = left.reshape(PIECES, 128, GROUP)
        holder[:, :, GROUP:] = right.reshape(PIECES, 128, 2 * GROUP)
    else:
        holder[...] = dot(a_t[...], grads[...]).astype(BF16).reshape(PIECES, 128, wide)
    columns = pl.ds(pl.multiple_of(step * wide, GROUP), wide)
    scatter_rows(me, 0, holder, targets, columns)
    q_sum[...] = jnp.sum(grads[:, :GROUP].astype(F32), 0, keepdims=True)
    v_sum[...] = jnp.sum(grads[:, 2 * GROUP :].astype(F32), 0, keepdims=True)


def attend_backward(scalars, base, steps, a_t, side, go, saved, gb, natural, deps=()):
    cross = side.dtype == BF16
    wide = 3 * GROUP
    with_out = gb is not None
    total = steps * wide + (D if with_out else 0)

    def block():
        return pl.BlockSpec((ROWS, GROUP), lambda i, s: (0, base + i))

    scratch = [
        pltpu.VMEM((D, ROWS), BF16),
        pltpu.VMEM((128, ROWS), F32),
        pltpu.VMEM((128, ROWS), F32),
        pltpu.VMEM((PIECES, 128, wide), BF16),
        pltpu.SemaphoreType.DMA((2,)),
    ]
    operands = [a_t, side]
    in_specs = [ANY, ANY if cross else whole((ROWS, ROWS))]
    if cross:
        scratch.append(pltpu.VMEM((D, ROWS), BF16))
    if with_out:
        out_rows = D // steps
        operands += [gb, saved[3]]
        in_specs += [whole((ROWS, D)), pl.BlockSpec((ROWS, out_rows), lambda i, s: (0, i))]
        scratch.append(pltpu.VMEM((out_rows // 128, 128, D), BF16))
    targets = [(PIECES, 128, total)] if natural else [(HALF, 128, total)] * 2
    return pl.pallas_call(
        skipping(functools.partial(attend_backward_body, cross, with_out, natural), 1, len(deps)),
        grid_spec=pltpu.PrefetchScalarGridSpec(
            num_scalar_prefetch=1,
            grid=(steps,),
            in_specs=[ANY] * len(deps)
            + in_specs
            + [block()] * 5
            + [pl.BlockSpec((1, ROWS, 4), lambda i, s: (base + i, 0, 0))],
            out_specs=[pl.BlockSpec((ROWS, wide), lambda i, s: (0, i))]
            + [whole(shape) for shape in targets]
            + [pl.BlockSpec((1, GROUP), lambda i, s: (0, i))] * 2,
            scratch_shapes=scratch,
        ),
        out_shape=[shaped((ROWS, steps * wide))]
        + [shaped(shape) for shape in targets]
        + [shaped((1, steps * GROUP), F32)] * 2,
        compiler_params=PARAMS,
        cost_estimate=cost(2 * ROWS * D * D * (1 + 5 * steps), 20e6, 4 * steps * ROWS * ROWS),
        name="cross_backward" if cross else "self_backward",
    )(scalars, *deps, *operands, go, *saved)


def project_back_body(layout, below_layout, counts, *refs):
    cross = below_layout is not None
    it = iter(refs)
    scalars = next(it)
    grads = [next(it) for _ in counts]
    gx, x_ref, gain = next(it), next(it), next(it)
    parts = [next(it) for _ in layout]
    if cross:
        below = [next(it) for _ in below_layout]
    gx_out, gain_sum, shift_sum = (next(it) for _ in range(3))
    if cross:
        genc, b_sum, gb_out, go = (next(it) for _ in range(4))
    da, weights, sems = (next(it) for _ in range(3))
    if cross:
        denc, out_weights, out_sems = (next(it) for _ in range(3))
    group = pl.program_id(0)
    me = scalars[0]

    @pl.when(group == 0)
    def _():
        start_all(qkv_copies(me, 0, layout, parts, weights, sems))
        if cross:
            start_all(out_copies(me, below_layout, below, out_weights, out_sems))

    @pl.when(group < GROUPS - 1)
    def _():
        start_all(qkv_copies(me, group + 1, layout, parts, weights, sems))

    wait_all(qkv_copies(me, group, layout, parts, weights, sems))

    def go_on(grad, opening):
        tile = weights[group % 2]
        if cross:
            from_q = dot_t(grad[:, :GROUP], tile[:, :GROUP])
            from_kv = dot_t(grad[:, GROUP:], tile[:, GROUP:])
            denc[...] = from_kv if opening else denc[...] + from_kv
        else:
            from_q = dot_t(grad[...], tile)
        da[...] = from_q if opening else da[...] + from_q

    @pl.when(group == 0)
    def _():
        go_on(grads[0], True)

    first = 0
    for grad, count in zip(grads, counts):

        @pl.when((group >= max(first, 1)) & (group < first + count))
        def _(grad=grad):
            go_on(grad, False)

        first += count

    @pl.when(group == GROUPS - 1)
    def _():
        back, gain_grad, shift_grad = norm_back(da[...], x_ref[...].astype(F32), gain[...])
        gain_sum[...] = gain_grad
        shift_sum[...] = shift_grad
        total = gx[...] + back
        gx_out[...] = total.astype(gx_out.dtype)
        if cross:
            genc[...] = denc[...].astype(BF16)
            gb = total.astype(BF16)
            gb_out[...] = gb
            b_sum[...] = jnp.sum(gb.astype(F32), 0, keepdims=True)
            wait_all(out_copies(me, below_layout, below, out_weights, out_sems))
            go[...] = dot_t(gb, out_weights[...]).astype(BF16)


def project_back(scalars, grads, gx, x, gain, held, below=None, deps=()):
    cross = below is not None
    wide = 3 * GROUP
    layout, parts = held
    counts = [grad.shape[1] // wide for grad in grads]
    starts = [sum(counts[:i]) for i in range(len(counts))]

    def grad_spec(start, count):
        return pl.BlockSpec((ROWS, wide), lambda g, s: (0, jnp.clip(g - start, 0, count - 1)))

    operands = [*grads, gx, x, gain, *parts]
    in_specs = [grad_spec(start, count) for start, count in zip(starts, counts)]
    in_specs += [whole((ROWS, D)), whole((ROWS, D)), whole((1, D))] + [ANY] * len(parts)
    out_shape = [shaped((ROWS, D), F32 if cross else BF16)] + [shaped((1, D), F32)] * 2
    scratch = [
        pltpu.VMEM((ROWS, D), F32),
        pltpu.VMEM((2, D, wide), BF16),
        pltpu.SemaphoreType.DMA((2, 3 * len(parts))),
    ]
    if cross:
        operands += [*below[1]]
        in_specs += [ANY] * len(below[1])
        out_shape += [shaped((ROWS, D)), shaped((1, D), F32)] + [shaped((ROWS, D))] * 2
        scratch += [
            pltpu.VMEM((ROWS, D), F32),
            pltpu.VMEM((D, D), BF16),
            pltpu.SemaphoreType.DMA((len(below[1]),)),
        ]
    return pl.pallas_call(
        skipping(
            functools.partial(
                project_back_body, layout, below[0] if cross else None, tuple(counts)
            ),
            1,
            len(deps),
        ),
        grid_spec=pltpu.PrefetchScalarGridSpec(
            num_scalar_prefetch=1,
            grid=(GROUPS,),
            in_specs=[ANY] * len(deps) + in_specs,
            out_specs=[whole(out.shape) for out in out_shape],
            scratch_shapes=scratch,
        ),
        out_shape=out_shape,
        compiler_params=PARAMS,
        cost_estimate=cost(2 * ROWS * D * D * (4 if cross else 3), 30e6),
        name="cross_project" if cross else "self_project",
    )(scalars, *deps, *operands)


def mlp_up_body(a_ref, go, w1, b1, active_out, slope_out, grad_w2):
    unit = dot(a_ref[...], w1[...]) + b1[...]
    square = unit * unit
    gate = 0.5 + 0.5 * jnp.tanh(unit * (GELU_A + GELU_B * square))
    value = unit * gate
    active = value.astype(BF16)
    active_out[...] = active
    slope = gate + value * (1.0 - gate) * (2.0 * GELU_A + 6.0 * GELU_B * square)
    slope_out[...] = slope.astype(BF16)
    grad_w2[...] = dot_a(active, go[...]).astype(BF16)


def mlp_up(a, go, w1, b1, deps=()):
    ff = w1.shape[1]

    def fixed(shape):
        return pl.BlockSpec(shape, lambda i: (0, 0), pipeline_mode=pl.Buffered(1))

    tall = pl.BlockSpec((ROWS, TILE), lambda i: (0, i))
    return pl.pallas_call(
        skipping(mlp_up_body, 0, len(deps)),
        grid=(ff // TILE,),
        in_specs=[ANY] * len(deps)
        + [
            fixed((ROWS, D)),
            fixed((ROWS, D)),
            pl.BlockSpec((D, TILE), lambda i: (0, i)),
            pl.BlockSpec((1, TILE), lambda i: (0, i)),
        ],
        out_specs=[tall, tall, pl.BlockSpec((TILE, D), lambda i: (i, 0))],
        out_shape=[shaped((ROWS, ff)), shaped((ROWS, ff)), shaped((ff, D))],
        compiler_params=PARAMS,
        cost_estimate=cost(2 * 2 * ROWS * D * ff, 60e6, ROWS * ff),
        name="mlp_up",
    )(*deps, a, go, w1, b1)


def row_tile_copies(me, layout, parts, step, slot, weights, sems):
    for (rank, first, count), part_ref in zip(layout, parts):
        target = weights.at[slot, pl.ds(first, count), :]
        if rank is None:
            rows = pl.ds(pl.multiple_of(place(me, step) * count, count), count)
            pltpu.make_async_copy(part_ref.at[rows, :], target, sems.at[slot]).start()
        else:

            @pl.when(step == rank)
            def _(part_ref=part_ref, target=target):
                pltpu.make_async_copy(part_ref, target, sems.at[slot]).start()


def wait_tile(slot, weights, sems):
    pltpu.make_async_copy(weights.at[slot], weights.at[slot], sems.at[slot]).wait()


def tile_of(step, scalars):
    return place(scalars[0], step)


def mlp_down_body(layout, below_layout, steps, *refs):
    it = iter(refs)
    scalars = next(it)
    a_t, go, slope, w1 = (next(it) for _ in range(4))
    x_hbm, gain = next(it), next(it)
    parts = [next(it) for _ in layout]
    below = [next(it) for _ in below_layout]
    grad_w1, b1_sum, gx_out, gb_out, ga, gain_sum, shift_sum, b_sum = (next(it) for _ in range(8))
    da, w2, sems, x_ref, out_weights, out_sems, sem = (next(it) for _ in range(7))
    step = pl.program_id(0)
    me = scalars[0]
    slot = step % 2

    @pl.when(step == 0)
    def _():
        row_tile_copies(me, layout, parts, 0, 0, w2, sems)
        da[...] = jnp.zeros_like(da)

    @pl.when(step == 1)
    def _():
        start_all(out_copies(me, below_layout, below, out_weights, out_sems))
        pltpu.make_async_copy(x_hbm, x_ref, sem.at[0]).start()

    @pl.when(step < steps - 1)
    def _():
        row_tile_copies(me, layout, parts, step + 1, 1 - slot, w2, sems)

    wait_tile(slot, w2, sems)
    grad_unit = (dot_t(go[...], w2[slot]) * slope[...].astype(F32)).astype(BF16)
    b1_sum[...] = jnp.sum(grad_unit.astype(F32), 0, keepdims=True)
    grad_w1[...] = dot(a_t[...], grad_unit).astype(BF16)
    da[...] += dot_t(grad_unit, w1[...])

    @pl.when(step == steps - 1)
    def _():
        pltpu.make_async_copy(x_hbm, x_ref, sem.at[0]).wait()
        back, gain_grad, shift_grad = norm_back(da[...], x_ref[...], gain[...])
        gain_sum[...] = gain_grad
        shift_sum[...] = shift_grad
        total = go[...].astype(F32) + back
        gx_out[...] = total
        gb = total.astype(BF16)
        gb_out[...] = gb
        b_sum[...] = jnp.sum(gb.astype(F32), 0, keepdims=True)
        wait_all(out_copies(me, below_layout, below, out_weights, out_sems))
        ga[...] = dot_t(gb, out_weights[...]).astype(BF16)


def mlp_down(scalars, a_t, go, slope, w1, x, gain, held, below, deps=()):
    ff = w1.shape[1]
    steps = ff // TILE
    layout, parts = held
    tall = pl.BlockSpec((ROWS, TILE), lambda i, s: (0, tile_of(i, s)))
    out_shape = [shaped((D, ff)), shaped((1, ff), F32), shaped((ROWS, D), F32)]
    out_shape += [shaped((ROWS, D))] * 2 + [shaped((1, D), F32)] * 3
    return pl.pallas_call(
        skipping(functools.partial(mlp_down_body, layout, below[0], steps), 1, len(deps)),
        grid_spec=pltpu.PrefetchScalarGridSpec(
            num_scalar_prefetch=1,
            grid=(steps,),
            in_specs=[ANY] * len(deps)
            + [whole((D, ROWS)), whole((ROWS, D)), tall, tall, ANY, whole((1, D))]
            + [ANY] * (len(parts) + len(below[1])),
            out_specs=[tall, pl.BlockSpec((1, TILE), lambda i, s: (0, tile_of(i, s)))]
            + [whole(out.shape) for out in out_shape[2:]],
            scratch_shapes=[
                pltpu.VMEM((ROWS, D), F32),
                pltpu.VMEM((2, TILE, D), BF16),
                pltpu.SemaphoreType.DMA((2,)),
                pltpu.VMEM((ROWS, D), F32),
                pltpu.VMEM((D, D), BF16),
                pltpu.SemaphoreType.DMA((len(below[1]),)),
                pltpu.SemaphoreType.DMA((1,)),
            ],
        ),
        out_shape=out_shape,
        compiler_params=PARAMS,
        cost_estimate=cost(3 * 2 * ROWS * D * ff, 60e6),
        name="mlp_down",
    )(scalars, *deps, a_t, go, slope, w1, x, gain, *parts, *below[1])


def mlp_out_body(layout, steps, *refs):
    it = iter(refs)
    scalars = next(it)
    me = scalars[0]
    active, x_hbm, vector = (next(it) for _ in range(3))
    parts = [next(it) for _ in layout]
    result = next(it)
    acc, w2, sems, x_ref, sem = (next(it) for _ in range(5))
    step = pl.program_id(0)
    slot = step % 2

    @pl.when(step == 0)
    def _():
        row_tile_copies(me, layout, parts, 0, 0, w2, sems)
        acc[...] = jnp.zeros_like(acc)

    @pl.when(step == 1)
    def _():
        pltpu.make_async_copy(x_hbm, x_ref, sem.at[0]).start()

    @pl.when(step < steps - 1)
    def _():
        row_tile_copies(me, layout, parts, step + 1, 1 - slot, w2, sems)

    wait_tile(slot, w2, sems)
    acc[...] += dot(active[...], w2[slot])

    @pl.when(step == steps - 1)
    def _():
        pltpu.make_async_copy(x_hbm, x_ref, sem.at[0]).wait()
        result[...] = (x_ref[...] + acc[...] + vector[...]).astype(BF16)


def mlp_out(scalars, active, x, vector, held, deps=()):
    ff = active.shape[1]
    steps = ff // TILE
    layout, parts = held
    return pl.pallas_call(
        skipping(functools.partial(mlp_out_body, layout, steps), 1, len(deps)),
        grid_spec=pltpu.PrefetchScalarGridSpec(
            num_scalar_prefetch=1,
            grid=(steps,),
            in_specs=[ANY] * len(deps)
            + [
                pl.BlockSpec((ROWS, TILE), lambda i, s: (0, tile_of(i, s))),
                ANY,
                whole((1, D)),
            ]
            + [ANY] * len(parts),
            out_specs=whole((ROWS, D)),
            scratch_shapes=[
                pltpu.VMEM((ROWS, D), F32),
                pltpu.VMEM((2, TILE, D), BF16),
                pltpu.SemaphoreType.DMA((2,)),
                pltpu.VMEM((ROWS, D), F32),
                pltpu.SemaphoreType.DMA((1,)),
            ],
        ),
        out_shape=shaped((ROWS, D)),
        compiler_params=PARAMS,
        cost_estimate=cost(2 * ROWS * D * ff, 40e6),
        name="mlp_out",
    )(scalars, *deps, active, x, vector, *parts)


def prepare_body(x_ref, gain, shift, seg_col, seg_row, pad_row, a_ref, a_t, bias):
    normed, _ = normalize(x_ref[...].astype(F32))
    values = (normed * gain[...] + shift[...]).astype(BF16)
    a_ref[...] = values
    a_t[...] = values.T
    bias[...] = jnp.full_like(bias, MASKED)
    build_self_bias(seg_col, seg_row, pad_row, bias)


def prepare(x, gain, shift, masks):
    return pl.pallas_call(
        prepare_body,
        out_shape=[shaped((ROWS, D)), shaped((D, ROWS)), shaped((ROWS, ROWS), F32)],
        compiler_params=PARAMS,
        name="prepare",
    )(x, gain, shift, *masks)


CORE, XBIT, YBIT = 1, 2, 4


def gather_vectors(ln_gain, self_vec, cross_vec, mlp_vec):
    sizes = [3 * ln_gain.shape[1], self_vec.shape[0], cross_vec.shape[0], mlp_vec.shape[0]]
    packed = jnp.concatenate([ln_gain.reshape(-1), self_vec, cross_vec, mlp_vec])
    every = lax.all_gather(packed, "shard").astype(F32)
    ends = [sum(sizes[: i + 1]) for i in range(4)]
    gains = every[:, : ends[0]].reshape(-1, 3, ln_gain.shape[1]).transpose(1, 0, 2)
    gains = gains.reshape(3, 1, D)
    return [gains] + [every[:, a:b].reshape(1, -1) for a, b in zip(ends[:3], ends[1:])]


def join_heads_body(factor, counts, *refs):
    *sources, target, out = refs
    group = 0
    for source, count in zip(sources, counts):
        for inner in range(count):
            for index in range(3):
                first = index * D + group * GROUP
                start = inner * 3 * GROUP + index * GROUP
                target[:, first : first + GROUP] = (
                    source[:, start : start + GROUP].astype(F32) * factor
                )
            group += 1
        if source.shape[1] > count * 3 * GROUP:
            out[...] = source[:, count * 3 * GROUP :].astype(F32) * factor


def join_heads(parts, factor):
    rows = parts[0].shape[0]
    wide = 3 * GROUP
    counts = [(p.shape[1] - (D if p.shape[1] % wide else 0)) // wide for p in parts]
    return pl.pallas_call(
        functools.partial(join_heads_body, factor, counts),
        out_shape=[shaped((rows, 3 * D), F32), shaped((rows, D), F32)],
        compiler_params=PARAMS,
        name="join_heads",
    )(*parts)


def swap(value, axis, bit):
    size = lax.axis_size(axis)
    return lax.ppermute(value, axis, [(i, i ^ bit) for i in range(size)])


def add(left, right):
    return (left.astype(F32) + right.astype(F32)).astype(BF16)


def spread(own, axis):
    by_x, by_y = yield [(own, "shard", XBIT), (own, "shard", YBIT)]
    size = own.shape[axis]
    half = size // 2
    low = lax.slice_in_dim(by_x, 0, half, axis=axis)
    high = lax.slice_in_dim(by_y, half, size, axis=axis)
    far = [(low, "shard", YBIT), (high, "shard", XBIT)]
    far = yield far + [(v, "shard", CORE) for v in (own, by_x, by_y)]
    last = yield [(far[0], "shard", CORE), (far[1], "shard", CORE)]
    layout = [(0, 0, size), (2, 0, size), (4, 0, size), (1, 0, size), (3, 0, size), (5, 0, size)]
    layout += [(6, 0, half), (6, half, half), (7, 0, half), (7, half, half)]
    return tuple(layout), [own, by_x, by_y, *far[2:], *far[:2], *last]


def over_copies(value):
    copies = lax.axis_size("rep")
    if copies == 1:
        return value
    odd = lax.axis_index("rep") % 2 == 1
    rows = value.shape[0] // 2
    low, high = value[:rows], value[rows:]
    (got,) = yield [(jnp.where(odd, low, high), "rep", 1)]
    total = add(jnp.where(odd, high, low), got)
    bit = 2
    while bit < copies:
        (got,) = yield [(total, "rep", bit)]
        total = add(total, got)
        bit *= 2
    (other,) = yield [(total, "rep", 1)]
    return jnp.concatenate([jnp.where(odd, other, total), jnp.where(odd, total, other)], 0)


def reduce(keep, send):
    half = keep.shape[2] // 2
    (got,) = yield [(send, "shard", CORE)]
    total = add(keep, got)
    sum_a, sum_b = total[..., :half], total[..., half:]
    got = yield [(sum_a[1::2], "shard", XBIT), (sum_b[2:], "shard", YBIT)]
    half_a, half_b = add(sum_a[0::2], got[0]), add(sum_b[:2], got[1])
    got = yield [(half_a[1], "shard", YBIT), (half_b[1], "shard", XBIT)]
    owned = [add(half_a[0], got[0]), add(half_b[0], got[1])]
    owned = yield from over_copies(jnp.concatenate(owned, 1))
    return owned


def sum_everywhere(vector):
    for axis in ("shard", "rep"):
        bit = 1
        while bit < lax.axis_size(axis):
            (got,) = yield [(vector, axis, bit)]
            vector = vector + got
            bit *= 2
    return vector


def tie_body(*_):
    pass


def tie(arrays, tokens):
    return pl.pallas_call(
        tie_body,
        in_specs=[ANY] * (len(arrays) + len(tokens)),
        out_specs=[ANY] * len(arrays),
        out_shape=[shaped(a.shape, a.dtype) for a in arrays],
        input_output_aliases={i: i for i in range(len(arrays))},
        name="tie",
    )(*arrays, *tokens)


class Flow:
    def __init__(self):
        self.active = {}
        self.results = {}
        self.deps = []

    def start(self, name, steps):
        self._request(name, steps, next(steps))

    def _request(self, name, steps, wanted):
        self.deps += [array for array, _, _ in wanted]
        self.active[name] = (steps, [swap(*want) for want in wanted])

    def meet(self, tokens, *names, more=()):
        names = [n for n in names if n in self.active]
        held = [array for n in names for array in self.active[n][1]]
        held = tie([*more, *held], tokens)
        more, held = held[: len(more)], held[len(more) :]
        self.deps += more
        for name in names:
            steps, arrays = self.active[name]
            arrays, held = held[: len(arrays)], held[len(arrays) :]
            self.deps += arrays
            try:
                self._request(name, steps, steps.send(arrays))
            except StopIteration as end:
                del self.active[name]
                self.results[name] = end.value
        return more

    def take(self):
        deps, self.deps = self.deps, []
        return deps


def part(vector, index):
    return vector[:, index * D : (index + 1) * D]


def forward_vectors(gains, vectors, layer):
    vector, below = vectors[layer], vectors[layer + 1]
    return (
        part(vector, 3),
        part(vector, 1),
        part(vector, 2),
        gains[layer + 1],
        part(below, 0),
    )


def gather(value):
    return lax.all_gather(value, "shard", axis=0, tiled=True)


def scattered(value):
    return lax.psum_scatter(value, "shard", scatter_dimension=0, tiled=True)


def ring_device(
    hidden,
    segments,
    pad_mask,
    encoder,
    src_len,
    grad_out,
    ln_gain,
    self_qkv,
    self_out,
    self_vec,
    cross_qkv,
    cross_out,
    cross_vec,
    fc_in,
    fc_out,
    mlp_vec,
):
    shards = lax.axis_size("shard")
    factor = 1.0 / math.sqrt(ROWS * lax.axis_size("rep") * shards)
    me = lax.axis_index("shard").astype(jnp.int32)
    scalars = jnp.stack([me, src_len[0]])
    flow = Flow()
    ff = fc_in.shape[1]

    gains, *vectors = gather_vectors(ln_gain, self_vec, cross_vec, mlp_vec)
    all_one = gather(jnp.concatenate([self_qkv, self_out], 1))
    all_two = gather(jnp.concatenate([cross_qkv, cross_out], 1))
    held_one, held_two = (WHOLE, [all_one]), (WHOLE, [all_two])
    all_in = gather(fc_in)
    rows = fc_out.shape[0] // 2
    low_out = gather(fc_out[:rows])
    flow.start("high", spread(fc_out[rows:], 0))
    encoded = encoder.reshape(ROWS, D)
    enc_t = encoded.T
    masks = (segments.reshape(ROWS, 1), segments.reshape(1, ROWS), pad_mask.reshape(1, ROWS))
    a_one, a_one_t, bias = prepare(hidden, gains[0], part(vectors[0], 0), masks)
    out_sum = jnp.sum(grad_out.astype(F32), 0)
    flow.take()
    flow.meet([a_one_t, enc_t], "high")
    x_one, a_two, a_two_t, *saved_one = attend_forward(
        scalars,
        hidden,
        a_one,
        bias,
        forward_vectors(gains, vectors, 0),
        held_one,
        deps=flow.take(),
    )
    flow.meet([a_two], "high")
    flow.meet([saved_one[4]], "high")
    layout, high_parts = flow.results["high"]
    layout = ((None, 0, rows),) + tuple((r, rows + first, count) for r, first, count in layout)
    held_out = (layout, [low_out, *high_parts])
    flow.take()
    x_two, a_three, a_three_t, *saved_two = attend_forward(
        scalars, x_one, a_two, encoded, forward_vectors(gains, vectors, 1), held_two
    )
    active, slope, grad_w2 = mlp_up(a_three, grad_out, all_in, part_from(vectors[2], 2))
    scattered_out = scattered(grad_w2)
    grad_w1, sum_fc, grad_two, gb_two, ga_two, gain_three, shift_three, out_two = mlp_down(
        scalars, a_three_t, grad_out, slope, all_in, x_two, gains[2], held_out, held_two
    )
    scattered_in = scattered(grad_w1)
    halves_two, *weights_two, q_two, v_two = attend_backward(
        scalars, 0, GROUPS, a_two_t, enc_t, ga_two, saved_two, gb_two, False
    )
    (scattered_out,) = flow.meet([v_two], more=[scattered_out])
    flow.start("out", over_copies(scattered_out))
    flow.start("cross", reduce(*weights_two))
    grad_one, gain_two, shift_two, grad_enc, out_one, gb_one, ga_one = project_back(
        scalars,
        [halves_two],
        grad_two,
        x_one,
        gains[1],
        held_two,
        held_one,
        deps=flow.take(),
    )
    flow.meet([gain_two], "cross", "out")
    early = [gain_three[0], shift_three[0], out_sum, sum_fc[0]]
    early += [gain_two[0], shift_two[0], q_two[0], v_two[0], out_two[0]]
    flow.start("early", sum_everywhere(jnp.concatenate(early)))
    grads_one, weights_one, q_one, v_one = attend_backward(
        scalars,
        0,
        GROUPS,
        a_one_t,
        bias,
        ga_one,
        saved_one,
        gb_one,
        True,
        deps=flow.take(),
    )
    (weights_one,) = flow.meet([v_one], "cross", "out", "early", more=[weights_one])
    scattered_one = scattered(weights_one)
    grad_hidden, gain_one, shift_one = project_back(
        scalars, [grads_one], grad_one, hidden, gains[0], held_one, deps=flow.take()
    )
    (scattered_in,) = flow.meet([gain_one], "cross", "out", "early", more=[scattered_in])
    flow.start("in", over_copies(scattered_in))
    late = [gain_one[0], shift_one[0], q_one[0], v_one[0], out_one[0]]
    flow.start("late", sum_everywhere(jnp.concatenate(late)))
    output = mlp_out(
        scalars, active, x_two, part(vectors[2], 1), held_out, deps=flow.take()
    )
    (scattered_one,) = flow.meet([output], "cross", "in", "early", "late", more=[scattered_one])
    flow.start("self", over_copies(scattered_one[0]))
    while flow.active:
        flow.meet(flow.take(), *flow.active)
    done = flow.results

    def own(vector):
        size = vector.shape[0] // shards
        return lax.dynamic_slice_in_dim(vector, me * size, size) * factor

    base = 3 * D + ff
    early, late = done["early"], done["late"]
    grad_gain = jnp.stack([own(late[:D]), own(early[base : base + D]), own(early[:D])], 0)
    return (
        output,
        grad_hidden,
        grad_enc.reshape(1, ROWS, D),
        grad_gain,
        *join_heads([done["self"]], factor),
        own(late[D:]),
        *join_heads([done["cross"]], factor),
        own(early[base + D :]),
        done["in"].astype(F32) * factor,
        done["out"].astype(F32) * factor,
        own(early[D:base]),
    )


def part_from(vector, index):
    return vector[:, index * D :]


def gather_device(
    hidden,
    segments,
    pad_mask,
    encoder,
    src_len,
    grad_out,
    ln_gain,
    self_qkv,
    self_out,
    self_vec,
    cross_qkv,
    cross_out,
    cross_vec,
    fc_in,
    fc_out,
    mlp_vec,
):
    shards = lax.axis_size("shard")
    factor = 1.0 / math.sqrt(ROWS * lax.axis_size("rep") * shards)
    scalars = jnp.stack([jnp.int32(0), src_len[0]])
    encoded = encoder.reshape(ROWS, D)
    enc_t = encoded.T
    gains, *vectors = gather_vectors(ln_gain, self_vec, cross_vec, mlp_vec)
    held_one = (WHOLE, [gather(jnp.concatenate([self_qkv, self_out], 1))])
    held_two = (WHOLE, [gather(jnp.concatenate([cross_qkv, cross_out], 1))])
    all_in, held_out = gather(fc_in), (WHOLE_ROWS, [gather(fc_out)])
    masks = (segments.reshape(ROWS, 1), segments.reshape(1, ROWS), pad_mask.reshape(1, ROWS))
    a_one, a_one_t, bias = prepare(hidden, gains[0], part(vectors[0], 0), masks)
    x_one, a_two, a_two_t, *saved_one = attend_forward(
        scalars, hidden, a_one, bias, forward_vectors(gains, vectors, 0), held_one
    )
    x_two, a_three, a_three_t, *saved_two = attend_forward(
        scalars, x_one, a_two, encoded, forward_vectors(gains, vectors, 1), held_two
    )
    active, slope, grad_w2 = mlp_up(a_three, grad_out, all_in, part_from(vectors[2], 2))
    grad_w1, sum_fc, grad_two, gb_two, ga_two, gain_three, shift_three, out_two = mlp_down(
        scalars, a_three_t, grad_out, slope, all_in, x_two, gains[2], held_out, held_two
    )
    halves_two, weights_two, q_two, v_two = attend_backward(
        scalars, 0, GROUPS, a_two_t, enc_t, ga_two, saved_two, gb_two, True
    )
    grad_one, gain_two, shift_two, grad_enc, out_one, gb_one, ga_one = project_back(
        scalars, [halves_two], grad_two, x_one, gains[1], held_two, held_one
    )
    halves_one, weights_one, q_one, v_one = attend_backward(
        scalars, 0, GROUPS, a_one_t, bias, ga_one, saved_one, gb_one, True
    )
    grad_hidden, gain_one, shift_one = project_back(
        scalars, [halves_one], grad_one, hidden, gains[0], held_one
    )
    output = mlp_out(scalars, active, x_two, part(vectors[2], 1), held_out)

    def summed(value):
        return lax.psum(scattered(value.astype(BF16)), "rep")

    def final(value):
        return summed(value).astype(F32) * factor

    ones = [shift_one[0], q_one[0], v_one[0], out_one[0]]
    twos = [shift_two[0], q_two[0], v_two[0], out_two[0]]
    threes = [shift_three[0], jnp.sum(grad_out.astype(F32), 0), sum_fc[0]]
    gain = jnp.concatenate([gain_one, gain_two, gain_three], 0)
    return (
        output,
        grad_hidden,
        grad_enc.reshape(1, ROWS, D),
        final(gain.T).T,
        *join_heads([summed(weights_one.reshape(D, -1))], factor),
        final(jnp.concatenate(ones)),
        *join_heads([summed(weights_two.reshape(D, -1))], factor),
        final(jnp.concatenate(twos)),
        final(grad_w1),
        final(grad_w2),
        final(jnp.concatenate(threes)),
    )


def per_device(*arrays):
    copies = lax.axis_size("rep")
    if lax.axis_size("shard") == PIECES and copies & (copies - 1) == 0:
        return ring_device(*arrays)
    return gather_device(*arrays)


def solution(mesh):
    placed = (
        P(("rep", "shard"), None),
        P(("rep", "shard")),
        P(("rep", "shard")),
        P(("rep", "shard"), None, None),
        P(("rep", "shard")),
        P(("rep", "shard"), None),
        P(None, "shard"),
        P("shard", None),
        P("shard", None),
        P("shard"),
        P("shard", None),
        P("shard", None),
        P("shard"),
        P("shard", None),
        P("shard", None),
        P("shard"),
    )
    return jax.shard_map(
        per_device,
        mesh=mesh,
        in_specs=placed,
        out_specs=(
            P(("rep", "shard"), None),
            P(("rep", "shard"), None),
            P(("rep", "shard"), None, None),
            P(None, "shard"),
            P("shard", None),
            P("shard", None),
            P("shard"),
            P("shard", None),
            P("shard", None),
            P("shard"),
            P("shard", None),
            P("shard", None),
            P("shard"),
        ),
        check_vma=False,
    )
```

```python
import functools
import math

import jax
import jax.numpy as jnp
from jax import lax
from jax.experimental import pallas as pl
from jax.experimental.pallas import tpu as pltpu
from jax.sharding import PartitionSpec as P

HEADS = 16
HEAD_DIM = 64
EPSILON = 1e-05
MASKED = -1e30
GELU_A = math.sqrt(2.0 / math.pi)
GELU_B = GELU_A * 0.044715

D = 1024
ROWS = 1024
GROUP = 256
GROUPS = 4
PIECES = 8
QBLOCK = 512
KBLOCK = 256
TILE = 1024
F32 = jnp.float32
BF16 = jnp.bfloat16
VMEM_LIMIT = 62 * 1024 * 1024


def dot(left, right):
    return jnp.dot(left, right, preferred_element_type=F32)


def dot_t(left, right):
    return lax.dot_general(left, right, (((1,), (1,)), ((), ())), preferred_element_type=F32)


def dot_a(left, right):
    return lax.dot_general(left, right, (((0,), (0,)), ((), ())), preferred_element_type=F32)


def normalize(values):
    center = jnp.mean(values, -1, keepdims=True)
    offset = values - center
    scale_inv = lax.rsqrt(jnp.mean(offset * offset, -1, keepdims=True) + EPSILON)
    return offset * scale_inv, scale_inv


def norm_back(grad, values, gain):
    normed, scale_inv = normalize(values)
    scaled = grad * gain
    back = scale_inv * (
        scaled
        - jnp.mean(scaled, -1, keepdims=True)
        - normed * jnp.mean(scaled * normed, -1, keepdims=True)
    )
    return back, jnp.sum(grad * normed, 0, keepdims=True), jnp.sum(grad, 0, keepdims=True)


def split_three(values):
    high = values.astype(BF16)
    rest = values - high.astype(F32)
    middle = rest.astype(BF16)
    return high, middle, (rest - middle.astype(F32)).astype(BF16)


def place(me, rank):
    return lax.bitwise_xor(me, rank)


WHOLE = ((None, 0, 4 * D),)
WHOLE_ROWS = ((None, 0, D),)


def shard_rows(me, rank, rows_each):
    if rank is None:
        return pl.ds(0, rows_each * PIECES)
    return pl.ds(pl.multiple_of(place(me, rank) * rows_each, rows_each), rows_each)


def qkv_copies(me, group, layout, parts, weights, sems):
    copies = []
    slot = group % 2
    for number, ((rank, first, count), part_ref) in enumerate(zip(layout, parts)):
        rows = shard_rows(me, rank, D // PIECES)
        for index in range(3):
            if first <= index * D < first + count:
                start = index * D - first + group * GROUP
                source = pl.ds(pl.multiple_of(start, GROUP), GROUP)
                copies.append(
                    pltpu.make_async_copy(
                        part_ref.at[:, source],
                        weights.at[slot, rows, pl.ds(index * GROUP, GROUP)],
                        sems.at[slot, number * 3 + index],
                    )
                )
    return copies


def out_copies(me, layout, parts, out_weights, sems):
    copies = []
    for number, ((rank, first, count), part_ref) in enumerate(zip(layout, parts)):
        if first <= 3 * D < first + count:
            rows = shard_rows(me, rank, D // PIECES)
            source = pl.ds(3 * D - first, D)
            copies.append(
                pltpu.make_async_copy(
                    part_ref.at[:, source], out_weights.at[rows, :], sems.at[number]
                )
            )
    return copies


def start_all(copies):
    for copy in copies:
        copy.start()


def wait_all(copies):
    for copy in copies:
        copy.wait()


def build_self_bias(seg_col, seg_row, pad_row, bias):
    for first in range(0, ROWS, QBLOCK):
        count = first + QBLOCK
        rows = first + lax.broadcasted_iota(jnp.int32, (QBLOCK, count), 0)
        cols = lax.broadcasted_iota(jnp.int32, (QBLOCK, count), 1)
        same = seg_col[first : first + QBLOCK, :] == seg_row[:, :count]
        real = (pad_row[:, :count] == 1) | (cols == rows)
        allowed = (cols <= rows) & same & real
        bias[first : first + QBLOCK, :count] = jnp.where(allowed, 0.0, MASKED)


def lanes_of(half):
    lane = lax.broadcasted_iota(jnp.int32, (1, 128), 1)
    mine = (lane < 64) if half == 0 else (lane >= 64)
    return lane, mine, (64 if half == 0 else 0)


def key_mask(shape, length):
    rows = lax.broadcasted_iota(jnp.int32, shape, 0)
    return jnp.where(rows < length, 0.0, MASKED).astype(BF16)


def forward_pair(query, key, value, length, bias, out_ref, log_ref, pair, causal):
    lane, _, _ = lanes_of(0)
    columns = slice(pair * 128, pair * 128 + 128)
    logs = [[], []]
    for first in range(0, ROWS, QBLOCK):
        count = first + QBLOCK if causal else key.shape[0]
        outs = []
        for half in range(2):
            _, mine, extra = lanes_of(half)
            q_block = query[first : first + QBLOCK]
            if causal:
                q_ext = jnp.where(mine, q_block, jnp.zeros_like(q_block))
                scores = dot_t(q_ext, key[:count]) + bias[first : first + QBLOCK, :count]
            else:
                q_ext = jnp.where(mine, q_block, (lane == extra).astype(BF16))
                k_ext = jnp.where(lane == extra, key_mask(key.shape, length), key)
                scores = dot_t(q_ext, k_ext)
            row_max = jnp.max(scores, 1, keepdims=True)
            weights = jnp.exp(scores - row_max).astype(BF16)
            v_ext = jnp.where(mine, value[:count], jnp.ones_like(value[:count]))
            mixed = dot(weights, v_ext)
            total = mixed[:, extra : extra + 1]
            outs.append((mixed, total))
            log_ref[0, first : first + QBLOCK, 2 * pair + half : 2 * pair + half + 1] = (
                row_max + jnp.log(total)
            )
        numerator = jnp.where(lane < 64, outs[0][0], outs[1][0])
        denominator = jnp.where(lane < 64, outs[0][1], outs[1][1])
        out_ref[first : first + QBLOCK, columns] = (numerator / denominator).astype(BF16)


def attend_forward_body(cross, layout, *refs):
    it = iter(refs)
    scalars = next(it)
    x_ref, a_ref, side = next(it), next(it), next(it)
    out_bias, q_bias, v_bias, gain, shift = (next(it) for _ in range(5))
    parts = [next(it) for _ in layout]
    x_out, next_a, next_t, q_ref, k_ref, v_ref, o_ref, log_ref = (next(it) for _ in range(8))
    weights, out_weights, sems, out_sems = (next(it) for _ in range(4))
    group = pl.program_id(0)
    me = scalars[0]
    length = scalars[1]

    @pl.when(group == 0)
    def _():
        start_all(qkv_copies(me, 0, layout, parts, weights, sems))
        start_all(out_copies(me, layout, parts, out_weights, out_sems))
        x_out[...] = x_ref[...].astype(F32) + out_bias[...]

    @pl.when(group < GROUPS - 1)
    def _():
        start_all(qkv_copies(me, group + 1, layout, parts, weights, sems))

    wait_all(qkv_copies(me, group, layout, parts, weights, sems))

    def block(index):
        return weights[group % 2, :, index * GROUP : (index + 1) * GROUP]

    kv_rows = side[...] if cross else a_ref[...]
    q_ref[...] = ((dot(a_ref[...], block(0)) + q_bias[...]) * 0.125).astype(BF16)
    k_ref[...] = dot(kv_rows, block(1)).astype(BF16)
    v_ref[...] = (dot(kv_rows, block(2)) + v_bias[...]).astype(BF16)
    for pair in range(2):
        columns = slice(pair * 128, pair * 128 + 128)
        forward_pair(
            q_ref[:, columns],
            k_ref[:, columns],
            v_ref[:, columns],
            length,
            side,
            o_ref,
            log_ref,
            pair,
            not cross,
        )

    @pl.when(group == 0)
    def _():
        wait_all(out_copies(me, layout, parts, out_weights, out_sems))

    rows = pl.ds(pl.multiple_of(group * GROUP, GROUP), GROUP)
    x_out[...] += dot(o_ref[...], out_weights[rows, :])

    @pl.when(group == GROUPS - 1)
    def _():
        normed, _ = normalize(x_out[...])
        values = (normed * gain[...] + shift[...]).astype(BF16)
        next_a[...] = values
        next_t[...] = values.T


def whole(shape):
    zeros = (0,) * len(shape)
    return pl.BlockSpec(shape, lambda *_: zeros, pipeline_mode=pl.Buffered(1))


def group_block(rows=ROWS):
    return pl.BlockSpec((rows, GROUP), lambda g, s: (0, g))


ANY = pl.BlockSpec(memory_space=pl.ANY)
PARAMS = pltpu.CompilerParams(vmem_limit_bytes=VMEM_LIMIT)


def shaped(shape, dtype=BF16):
    return jax.ShapeDtypeStruct(shape, dtype)


def skipping(body, leading, count):
    def run(*refs):
        body(*refs[:leading], *refs[leading + count :])

    return run


def cost(flops, nbytes, exps=0):
    return pl.CostEstimate(flops=int(flops), bytes_accessed=int(nbytes), transcendentals=int(exps))


def attend_forward(scalars, x, a, side, vectors, held, deps=()):
    cross = side.dtype == BF16
    layout, parts = held
    return pl.pallas_call(
        skipping(functools.partial(attend_forward_body, cross, layout), 1, len(deps)),
        grid_spec=pltpu.PrefetchScalarGridSpec(
            num_scalar_prefetch=1,
            grid=(GROUPS,),
            in_specs=[ANY] * len(deps)
            + [whole((ROWS, D))] * 3
            + [whole((1, D))]
            + [group_block(1)] * 2
            + [whole((1, D))] * 2
            + [ANY] * len(parts),
            out_specs=[whole((ROWS, D))] * 3
            + [group_block()] * 4
            + [pl.BlockSpec((1, ROWS, 4), lambda g, s: (g, 0, 0))],
            scratch_shapes=[
                pltpu.VMEM((2, D, 3 * GROUP), BF16),
                pltpu.VMEM((D, D), BF16),
                pltpu.SemaphoreType.DMA((2, 3 * len(parts))),
                pltpu.SemaphoreType.DMA((len(parts),)),
            ],
        ),
        out_shape=[shaped((ROWS, D), F32), shaped((ROWS, D)), shaped((D, ROWS))]
        + [shaped((ROWS, D))] * 4
        + [shaped((GROUPS, ROWS, 4), F32)],
        compiler_params=PARAMS,
        cost_estimate=cost(2 * ROWS * D * D * (4 + 8), 30e6, HEADS * ROWS * ROWS),
        name="cross_forward" if cross else "self_forward",
    )(scalars, *deps, x, a, side, *vectors, *parts)


def backward_pair(refs, go_ref, length, bias, accs, pair, causal):
    q_ref, k_ref, v_ref, o_ref, log_ref = refs
    grads, dk_acc, dv_acc = accs
    columns = slice(pair * 128, pair * 128 + 128)
    query, key, value = q_ref[:, columns], k_ref[:, columns], v_ref[:, columns]
    go = go_ref[:, columns]
    q_turned, go_turned = query.T, go.T
    product = go.astype(F32) * o_ref[:, columns].astype(F32)
    zeros = jnp.zeros_like(query)
    q_ext, go_ext, k_ext, v_ext, k_own = [], [], [], [], []
    for half in range(2):
        lane, mine, extra = lanes_of(half)
        delta = jnp.sum(jnp.where(mine, product, 0.0), 1, keepdims=True)
        logs = log_ref[0, :, 2 * pair + half : 2 * pair + half + 1]
        k_own.append(jnp.where(mine, key, zeros))

        def with_rows(base, column, last):
            high, middle, low = split_three(-column)
            filled = jnp.where(lane == extra, high, jnp.where(lane == extra + 1, middle, zeros))
            filled = jnp.where(lane == extra + 2, low, filled)
            filled = jnp.where(lane == extra + 3, last, filled)
            return jnp.where(mine, base, filled)

        ones = ((lane >= extra) & (lane < extra + 3)).astype(BF16)
        one = jnp.ones_like(query)
        q_ext.append(with_rows(query, logs, zeros if causal else one))
        go_ext.append(with_rows(go, delta, zeros))
        keys = jnp.where(mine, key, ones)
        if not causal:
            keys = jnp.where(lane == extra + 3, key_mask(key.shape, length), keys)
        k_ext.append(keys)
        v_ext.append(jnp.where(mine, value, ones))
    last_first = ROWS - KBLOCK
    for first in range(last_first, -1, -KBLOCK):
        rows = slice(first, first + KBLOCK)
        count = first + KBLOCK if causal else key.shape[0]
        grads_q = []
        for half in range(2):
            scores = dot_t(q_ext[half][rows], k_ext[half][:count])
            if causal:
                scores = scores + bias[rows, :count]
            weights = jnp.exp(scores)
            grad_weights = dot_t(go_ext[half][rows], v_ext[half][:count])
            grad_scores = (weights * grad_weights).astype(BF16)
            grads_q.append(dot(grad_scores, k_own[half][:count]))
            dims = slice(64 * half, 64 * half + 64)
            grad_value = dot(go_turned[dims, rows], weights.astype(BF16))
            grad_key = dot(q_turned[dims, rows], grad_scores)
            if first == last_first:
                dv_acc[dims, :] = grad_value
                dk_acc[dims, :] = grad_key
            else:
                dv_acc[dims, :count] += grad_value
                dk_acc[dims, :count] += grad_key
        grads[rows, columns] = (grads_q[0] + grads_q[1]).astype(BF16) * 0.125
    for index, total in ((1, dk_acc), (2, dv_acc)):
        first = index * GROUP + pair * 128
        grads[:, first : first + 128] = total[...].astype(BF16).T


HALF = PIECES // 2


def scatter_rows(me, base, holder, targets, columns):
    shards = holder.shape[0]
    if len(targets) == 1:
        for index in range(shards):
            targets[0][base + index, :, columns] = holder[index]
        return
    keep, send = targets
    for index in range(shards // 2):
        if shards == PIECES:
            slot, pair = index, place(index, me // 2) * 2
        else:
            slot, pair = place(base // 2 + index, me // 2), 2 * index
        keep[slot, :, columns] = holder[pair + me % 2]
        send[slot, :, columns] = holder[pair + (1 - me % 2)]


def attend_backward_body(cross, with_out, natural, *refs):
    it = iter(refs)
    scalars = next(it)
    a_hbm = next(it)
    enc_hbm = next(it) if cross else None
    bias = None if cross else next(it)
    gb, o_rows = (next(it), next(it)) if with_out else (None, None)
    go, q_ref, k_ref, v_ref, o_ref, log_ref = (next(it) for _ in range(6))
    grads = next(it)
    targets = [next(it)] if natural else [next(it), next(it)]
    q_sum, v_sum = next(it), next(it)
    a_t, dk_acc, dv_acc, holder, sem = (next(it) for _ in range(5))
    enc_t = next(it) if cross else None
    holder_out = next(it) if with_out else None
    step = pl.program_id(0)
    me = scalars[0]
    wide = 3 * GROUP

    def loads():
        copies = [pltpu.make_async_copy(a_hbm, a_t, sem.at[0])]
        if cross:
            copies.append(pltpu.make_async_copy(enc_hbm, enc_t, sem.at[1]))
        return copies

    @pl.when(step == 0)
    def _():
        start_all(loads())

    if with_out:
        shards = o_rows.shape[1] // 128
        holder_out[...] = dot(o_rows[...].T, gb[...]).astype(BF16).reshape(shards, 128, D)
        first = targets[0].shape[2] - D
        scatter_rows(me, step * shards, holder_out, targets, slice(first, first + D))
    for pair in range(2):
        backward_pair(
            (q_ref, k_ref, v_ref, o_ref, log_ref),
            go,
            scalars[1],
            bias,
            (grads, dk_acc, dv_acc),
            pair,
            not cross,
        )

    @pl.when(step == 0)
    def _():
        wait_all(loads())

    if cross:
        left = dot(a_t[...], grads[:, :GROUP]).astype(BF16)
        right = dot(enc_t[...], grads[:, GROUP:]).astype(BF16)
        holder[:, :, :GROUP] = left.reshape(PIECES, 128, GROUP)
        holder[:, :, GROUP:] = right.reshape(PIECES, 128, 2 * GROUP)
    else:
        holder[...] = dot(a_t[...], grads[...]).astype(BF16).reshape(PIECES, 128, wide)
    columns = pl.ds(pl.multiple_of(step * wide, GROUP), wide)
    scatter_rows(me, 0, holder, targets, columns)
    q_sum[...] = jnp.sum(grads[:, :GROUP].astype(F32), 0, keepdims=True)
    v_sum[...] = jnp.sum(grads[:, 2 * GROUP :].astype(F32), 0, keepdims=True)


def attend_backward(scalars, base, steps, a_t, side, go, saved, gb, natural, deps=()):
    cross = side.dtype == BF16
    wide = 3 * GROUP
    with_out = gb is not None
    total = steps * wide + (D if with_out else 0)

    def block():
        return pl.BlockSpec((ROWS, GROUP), lambda i, s: (0, base + i))

    scratch = [
        pltpu.VMEM((D, ROWS), BF16),
        pltpu.VMEM((128, ROWS), F32),
        pltpu.VMEM((128, ROWS), F32),
        pltpu.VMEM((PIECES, 128, wide), BF16),
        pltpu.SemaphoreType.DMA((2,)),
    ]
    operands = [a_t, side]
    in_specs = [ANY, ANY if cross else whole((ROWS, ROWS))]
    if cross:
        scratch.append(pltpu.VMEM((D, ROWS), BF16))
    if with_out:
        out_rows = D // steps
        operands += [gb, saved[3]]
        in_specs += [whole((ROWS, D)), pl.BlockSpec((ROWS, out_rows), lambda i, s: (0, i))]
        scratch.append(pltpu.VMEM((out_rows // 128, 128, D), BF16))
    targets = [(PIECES, 128, total)] if natural else [(HALF, 128, total)] * 2
    return pl.pallas_call(
        skipping(functools.partial(attend_backward_body, cross, with_out, natural), 1, len(deps)),
        grid_spec=pltpu.PrefetchScalarGridSpec(
            num_scalar_prefetch=1,
            grid=(steps,),
            in_specs=[ANY] * len(deps)
            + in_specs
            + [block()] * 5
            + [pl.BlockSpec((1, ROWS, 4), lambda i, s: (base + i, 0, 0))],
            out_specs=[pl.BlockSpec((ROWS, wide), lambda i, s: (0, i))]
            + [whole(shape) for shape in targets]
            + [pl.BlockSpec((1, GROUP), lambda i, s: (0, i))] * 2,
            scratch_shapes=scratch,
        ),
        out_shape=[shaped((ROWS, steps * wide))]
        + [shaped(shape) for shape in targets]
        + [shaped((1, steps * GROUP), F32)] * 2,
        compiler_params=PARAMS,
        cost_estimate=cost(2 * ROWS * D * D * (1 + 5 * steps), 20e6, 4 * steps * ROWS * ROWS),
        name="cross_backward" if cross else "self_backward",
    )(scalars, *deps, *operands, go, *saved)


def project_back_body(layout, below_layout, counts, *refs):
    cross = below_layout is not None
    it = iter(refs)
    scalars = next(it)
    grads = [next(it) for _ in counts]
    gx, x_ref, gain = next(it), next(it), next(it)
    parts = [next(it) for _ in layout]
    if cross:
        below = [next(it) for _ in below_layout]
    gx_out, gain_sum, shift_sum = (next(it) for _ in range(3))
    if cross:
        genc, b_sum, gb_out, go = (next(it) for _ in range(4))
    da, weights, sems = (next(it) for _ in range(3))
    if cross:
        denc, out_weights, out_sems = (next(it) for _ in range(3))
    group = pl.program_id(0)
    me = scalars[0]

    @pl.when(group == 0)
    def _():
        start_all(qkv_copies(me, 0, layout, parts, weights, sems))
        if cross:
            start_all(out_copies(me, below_layout, below, out_weights, out_sems))

    @pl.when(group < GROUPS - 1)
    def _():
        start_all(qkv_copies(me, group + 1, layout, parts, weights, sems))

    wait_all(qkv_copies(me, group, layout, parts, weights, sems))

    def go_on(grad, opening):
        tile = weights[group % 2]
        if cross:
            from_q = dot_t(grad[:, :GROUP], tile[:, :GROUP])
            from_kv = dot_t(grad[:, GROUP:], tile[:, GROUP:])
            denc[...] = from_kv if opening else denc[...] + from_kv
        else:
            from_q = dot_t(grad[...], tile)
        da[...] = from_q if opening else da[...] + from_q

    @pl.when(group == 0)
    def _():
        go_on(grads[0], True)

    first = 0
    for grad, count in zip(grads, counts):

        @pl.when((group >= max(first, 1)) & (group < first + count))
        def _(grad=grad):
            go_on(grad, False)

        first += count

    @pl.when(group == GROUPS - 1)
    def _():
        back, gain_grad, shift_grad = norm_back(da[...], x_ref[...].astype(F32), gain[...])
        gain_sum[...] = gain_grad
        shift_sum[...] = shift_grad
        total = gx[...] + back
        gx_out[...] = total.astype(gx_out.dtype)
        if cross:
            genc[...] = denc[...].astype(BF16)
            gb = total.astype(BF16)
            gb_out[...] = gb
            b_sum[...] = jnp.sum(gb.astype(F32), 0, keepdims=True)
            wait_all(out_copies(me, below_layout, below, out_weights, out_sems))
            go[...] = dot_t(gb, out_weights[...]).astype(BF16)


def project_back(scalars, grads, gx, x, gain, held, below=None, deps=()):
    cross = below is not None
    wide = 3 * GROUP
    layout, parts = held
    counts = [grad.shape[1] // wide for grad in grads]
    starts = [sum(counts[:i]) for i in range(len(counts))]

    def grad_spec(start, count):
        return pl.BlockSpec((ROWS, wide), lambda g, s: (0, jnp.clip(g - start, 0, count - 1)))

    operands = [*grads, gx, x, gain, *parts]
    in_specs = [grad_spec(start, count) for start, count in zip(starts, counts)]
    in_specs += [whole((ROWS, D)), whole((ROWS, D)), whole((1, D))] + [ANY] * len(parts)
    out_shape = [shaped((ROWS, D), F32 if cross else BF16)] + [shaped((1, D), F32)] * 2
    scratch = [
        pltpu.VMEM((ROWS, D), F32),
        pltpu.VMEM((2, D, wide), BF16),
        pltpu.SemaphoreType.DMA((2, 3 * len(parts))),
    ]
    if cross:
        operands += [*below[1]]
        in_specs += [ANY] * len(below[1])
        out_shape += [shaped((ROWS, D)), shaped((1, D), F32)] + [shaped((ROWS, D))] * 2
        scratch += [
            pltpu.VMEM((ROWS, D), F32),
            pltpu.VMEM((D, D), BF16),
            pltpu.SemaphoreType.DMA((len(below[1]),)),
        ]
    return pl.pallas_call(
        skipping(
            functools.partial(
                project_back_body, layout, below[0] if cross else None, tuple(counts)
            ),
            1,
            len(deps),
        ),
        grid_spec=pltpu.PrefetchScalarGridSpec(
            num_scalar_prefetch=1,
            grid=(GROUPS,),
            in_specs=[ANY] * len(deps) + in_specs,
            out_specs=[whole(out.shape) for out in out_shape],
            scratch_shapes=scratch,
        ),
        out_shape=out_shape,
        compiler_params=PARAMS,
        cost_estimate=cost(2 * ROWS * D * D * (4 if cross else 3), 30e6),
        name="cross_project" if cross else "self_project",
    )(scalars, *deps, *operands)


def mlp_up_body(a_ref, go, w1, b1, active_out, slope_out, grad_w2):
    unit = dot(a_ref[...], w1[...]) + b1[...]
    square = unit * unit
    gate = 0.5 + 0.5 * jnp.tanh(unit * (GELU_A + GELU_B * square))
    value = unit * gate
    active = value.astype(BF16)
    active_out[...] = active
    slope = gate + value * (1.0 - gate) * (2.0 * GELU_A + 6.0 * GELU_B * square)
    slope_out[...] = slope.astype(BF16)
    grad_w2[...] = dot_a(active, go[...]).astype(BF16)


def mlp_up(a, go, w1, b1, deps=()):
    ff = w1.shape[1]

    def fixed(shape):
        return pl.BlockSpec(shape, lambda i: (0, 0), pipeline_mode=pl.Buffered(1))

    tall = pl.BlockSpec((ROWS, TILE), lambda i: (0, i))
    return pl.pallas_call(
        skipping(mlp_up_body, 0, len(deps)),
        grid=(ff // TILE,),
        in_specs=[ANY] * len(deps)
        + [
            fixed((ROWS, D)),
            fixed((ROWS, D)),
            pl.BlockSpec((D, TILE), lambda i: (0, i)),
            pl.BlockSpec((1, TILE), lambda i: (0, i)),
        ],
        out_specs=[tall, tall, pl.BlockSpec((TILE, D), lambda i: (i, 0))],
        out_shape=[shaped((ROWS, ff)), shaped((ROWS, ff)), shaped((ff, D))],
        compiler_params=PARAMS,
        cost_estimate=cost(2 * 2 * ROWS * D * ff, 60e6, ROWS * ff),
        name="mlp_up",
    )(*deps, a, go, w1, b1)


def row_tile_copies(me, layout, parts, step, slot, weights, sems):
    for (rank, first, count), part_ref in zip(layout, parts):
        target = weights.at[slot, pl.ds(first, count), :]
        if rank is None:
            rows = pl.ds(pl.multiple_of(place(me, step) * count, count), count)
            pltpu.make_async_copy(part_ref.at[rows, :], target, sems.at[slot]).start()
        else:

            @pl.when(step == rank)
            def _(part_ref=part_ref, target=target):
                pltpu.make_async_copy(part_ref, target, sems.at[slot]).start()


def wait_tile(slot, weights, sems):
    pltpu.make_async_copy(weights.at[slot], weights.at[slot], sems.at[slot]).wait()


def tile_of(step, scalars):
    return place(scalars[0], step)


def mlp_down_body(layout, below_layout, steps, *refs):
    it = iter(refs)
    scalars = next(it)
    a_t, go, slope, w1 = (next(it) for _ in range(4))
    x_hbm, gain = next(it), next(it)
    parts = [next(it) for _ in layout]
    below = [next(it) for _ in below_layout]
    grad_w1, b1_sum, gx_out, gb_out, ga, gain_sum, shift_sum, b_sum = (next(it) for _ in range(8))
    da, w2, sems, x_ref, out_weights, out_sems, sem = (next(it) for _ in range(7))
    step = pl.program_id(0)
    me = scalars[0]
    slot = step % 2

    @pl.when(step == 0)
    def _():
        row_tile_copies(me, layout, parts, 0, 0, w2, sems)
        da[...] = jnp.zeros_like(da)

    @pl.when(step == 1)
    def _():
        start_all(out_copies(me, below_layout, below, out_weights, out_sems))
        pltpu.make_async_copy(x_hbm, x_ref, sem.at[0]).start()

    @pl.when(step < steps - 1)
    def _():
        row_tile_copies(me, layout, parts, step + 1, 1 - slot, w2, sems)

    wait_tile(slot, w2, sems)
    grad_unit = (dot_t(go[...], w2[slot]) * slope[...].astype(F32)).astype(BF16)
    b1_sum[...] = jnp.sum(grad_unit.astype(F32), 0, keepdims=True)
    grad_w1[...] = dot(a_t[...], grad_unit).astype(BF16)
    da[...] += dot_t(grad_unit, w1[...])

    @pl.when(step == steps - 1)
    def _():
        pltpu.make_async_copy(x_hbm, x_ref, sem.at[0]).wait()
        back, gain_grad, shift_grad = norm_back(da[...], x_ref[...], gain[...])
        gain_sum[...] = gain_grad
        shift_sum[...] = shift_grad
        total = go[...].astype(F32) + back
        gx_out[...] = total
        gb = total.astype(BF16)
        gb_out[...] = gb
        b_sum[...] = jnp.sum(gb.astype(F32), 0, keepdims=True)
        wait_all(out_copies(me, below_layout, below, out_weights, out_sems))
        ga[...] = dot_t(gb, out_weights[...]).astype(BF16)


def mlp_down(scalars, a_t, go, slope, w1, x, gain, held, below, deps=()):
    ff = w1.shape[1]
    steps = ff // TILE
    layout, parts = held
    tall = pl.BlockSpec((ROWS, TILE), lambda i, s: (0, tile_of(i, s)))
    out_shape = [shaped((D, ff)), shaped((1, ff), F32), shaped((ROWS, D), F32)]
    out_shape += [shaped((ROWS, D))] * 2 + [shaped((1, D), F32)] * 3
    return pl.pallas_call(
        skipping(functools.partial(mlp_down_body, layout, below[0], steps), 1, len(deps)),
        grid_spec=pltpu.PrefetchScalarGridSpec(
            num_scalar_prefetch=1,
            grid=(steps,),
            in_specs=[ANY] * len(deps)
            + [whole((D, ROWS)), whole((ROWS, D)), tall, tall, ANY, whole((1, D))]
            + [ANY] * (len(parts) + len(below[1])),
            out_specs=[tall, pl.BlockSpec((1, TILE), lambda i, s: (0, tile_of(i, s)))]
            + [whole(out.shape) for out in out_shape[2:]],
            scratch_shapes=[
                pltpu.VMEM((ROWS, D), F32),
                pltpu.VMEM((2, TILE, D), BF16),
                pltpu.SemaphoreType.DMA((2,)),
                pltpu.VMEM((ROWS, D), F32),
                pltpu.VMEM((D, D), BF16),
                pltpu.SemaphoreType.DMA((len(below[1]),)),
                pltpu.SemaphoreType.DMA((1,)),
            ],
        ),
        out_shape=out_shape,
        compiler_params=PARAMS,
        cost_estimate=cost(3 * 2 * ROWS * D * ff, 60e6),
        name="mlp_down",
    )(scalars, *deps, a_t, go, slope, w1, x, gain, *parts, *below[1])


def mlp_out_body(layout, steps, *refs):
    it = iter(refs)
    scalars = next(it)
    me = scalars[0]
    active, x_hbm, vector = (next(it) for _ in range(3))
    parts = [next(it) for _ in layout]
    result = next(it)
    acc, w2, sems, x_ref, sem = (next(it) for _ in range(5))
    step = pl.program_id(0)
    slot = step % 2

    @pl.when(step == 0)
    def _():
        row_tile_copies(me, layout, parts, 0, 0, w2, sems)
        acc[...] = jnp.zeros_like(acc)

    @pl.when(step == 1)
    def _():
        pltpu.make_async_copy(x_hbm, x_ref, sem.at[0]).start()

    @pl.when(step < steps - 1)
    def _():
        row_tile_copies(me, layout, parts, step + 1, 1 - slot, w2, sems)

    wait_tile(slot, w2, sems)
    acc[...] += dot(active[...], w2[slot])

    @pl.when(step == steps - 1)
    def _():
        pltpu.make_async_copy(x_hbm, x_ref, sem.at[0]).wait()
        result[...] = (x_ref[...] + acc[...] + vector[...]).astype(BF16)


def mlp_out(scalars, active, x, vector, held, deps=()):
    ff = active.shape[1]
    steps = ff // TILE
    layout, parts = held
    return pl.pallas_call(
        skipping(functools.partial(mlp_out_body, layout, steps), 1, len(deps)),
        grid_spec=pltpu.PrefetchScalarGridSpec(
            num_scalar_prefetch=1,
            grid=(steps,),
            in_specs=[ANY] * len(deps)
            + [
                pl.BlockSpec((ROWS, TILE), lambda i, s: (0, tile_of(i, s))),
                ANY,
                whole((1, D)),
            ]
            + [ANY] * len(parts),
            out_specs=whole((ROWS, D)),
            scratch_shapes=[
                pltpu.VMEM((ROWS, D), F32),
                pltpu.VMEM((2, TILE, D), BF16),
                pltpu.SemaphoreType.DMA((2,)),
                pltpu.VMEM((ROWS, D), F32),
                pltpu.SemaphoreType.DMA((1,)),
            ],
        ),
        out_shape=shaped((ROWS, D)),
        compiler_params=PARAMS,
        cost_estimate=cost(2 * ROWS * D * ff, 40e6),
        name="mlp_out",
    )(scalars, *deps, active, x, vector, *parts)


def prepare_body(x_ref, gain, shift, seg_col, seg_row, pad_row, a_ref, a_t, bias):
    normed, _ = normalize(x_ref[...].astype(F32))
    values = (normed * gain[...] + shift[...]).astype(BF16)
    a_ref[...] = values
    a_t[...] = values.T
    bias[...] = jnp.full_like(bias, MASKED)
    build_self_bias(seg_col, seg_row, pad_row, bias)


def prepare(x, gain, shift, masks):
    return pl.pallas_call(
        prepare_body,
        out_shape=[shaped((ROWS, D)), shaped((D, ROWS)), shaped((ROWS, ROWS), F32)],
        compiler_params=PARAMS,
        name="prepare",
    )(x, gain, shift, *masks)


CORE, XBIT, YBIT = 1, 2, 4


def gather_vectors(ln_gain, self_vec, cross_vec, mlp_vec):
    sizes = [3 * ln_gain.shape[1], self_vec.shape[0], cross_vec.shape[0], mlp_vec.shape[0]]
    packed = jnp.concatenate([ln_gain.reshape(-1), self_vec, cross_vec, mlp_vec])
    every = lax.all_gather(packed, "shard").astype(F32)
    ends = [sum(sizes[: i + 1]) for i in range(4)]
    gains = every[:, : ends[0]].reshape(-1, 3, ln_gain.shape[1]).transpose(1, 0, 2)
    gains = gains.reshape(3, 1, D)
    return [gains] + [every[:, a:b].reshape(1, -1) for a, b in zip(ends[:3], ends[1:])]


def join_heads_body(factor, counts, *refs):
    *sources, target, out = refs
    group = 0
    for source, count in zip(sources, counts):
        for inner in range(count):
            for index in range(3):
                first = index * D + group * GROUP
                start = inner * 3 * GROUP + index * GROUP
                target[:, first : first + GROUP] = (
                    source[:, start : start + GROUP].astype(F32) * factor
                )
            group += 1
        if source.shape[1] > count * 3 * GROUP:
            out[...] = source[:, count * 3 * GROUP :].astype(F32) * factor


def join_heads(parts, factor):
    rows = parts[0].shape[0]
    wide = 3 * GROUP
    counts = [(p.shape[1] - (D if p.shape[1] % wide else 0)) // wide for p in parts]
    return pl.pallas_call(
        functools.partial(join_heads_body, factor, counts),
        out_shape=[shaped((rows, 3 * D), F32), shaped((rows, D), F32)],
        compiler_params=PARAMS,
        name="join_heads",
    )(*parts)


def swap(value, axis, bit):
    size = lax.axis_size(axis)
    return lax.ppermute(value, axis, [(i, i ^ bit) for i in range(size)])


def add(left, right):
    return (left.astype(F32) + right.astype(F32)).astype(BF16)


def spread(own, axis):
    by_x, by_y = yield [(own, "shard", XBIT), (own, "shard", YBIT)]
    size = own.shape[axis]
    half = size // 2
    low = lax.slice_in_dim(by_x, 0, half, axis=axis)
    high = lax.slice_in_dim(by_y, half, size, axis=axis)
    far = [(low, "shard", YBIT), (high, "shard", XBIT)]
    far = yield far + [(v, "shard", CORE) for v in (own, by_x, by_y)]
    last = yield [(far[0], "shard", CORE), (far[1], "shard", CORE)]
    layout = [(0, 0, size), (2, 0, size), (4, 0, size), (1, 0, size), (3, 0, size), (5, 0, size)]
    layout += [(6, 0, half), (6, half, half), (7, 0, half), (7, half, half)]
    return tuple(layout), [own, by_x, by_y, *far[2:], *far[:2], *last]


def over_copies(value):
    copies = lax.axis_size("rep")
    if copies == 1:
        return value
    odd = lax.axis_index("rep") % 2 == 1
    rows = value.shape[0] // 2
    low, high = value[:rows], value[rows:]
    (got,) = yield [(jnp.where(odd, low, high), "rep", 1)]
    total = add(jnp.where(odd, high, low), got)
    bit = 2
    while bit < copies:
        (got,) = yield [(total, "rep", bit)]
        total = add(total, got)
        bit *= 2
    (other,) = yield [(total, "rep", 1)]
    return jnp.concatenate([jnp.where(odd, other, total), jnp.where(odd, total, other)], 0)


def reduce(keep, send):
    half = keep.shape[2] // 2
    (got,) = yield [(send, "shard", CORE)]
    total = add(keep, got)
    sum_a, sum_b = total[..., :half], total[..., half:]
    got = yield [(sum_a[1::2], "shard", XBIT), (sum_b[2:], "shard", YBIT)]
    half_a, half_b = add(sum_a[0::2], got[0]), add(sum_b[:2], got[1])
    got = yield [(half_a[1], "shard", YBIT), (half_b[1], "shard", XBIT)]
    owned = [add(half_a[0], got[0]), add(half_b[0], got[1])]
    owned = yield from over_copies(jnp.concatenate(owned, 1))
    return owned


def sum_everywhere(vector):
    for axis in ("shard", "rep"):
        bit = 1
        while bit < lax.axis_size(axis):
            (got,) = yield [(vector, axis, bit)]
            vector = vector + got
            bit *= 2
    return vector


def tie_body(*_):
    pass


def tie(arrays, tokens):
    return pl.pallas_call(
        tie_body,
        in_specs=[ANY] * (len(arrays) + len(tokens)),
        out_specs=[ANY] * len(arrays),
        out_shape=[shaped(a.shape, a.dtype) for a in arrays],
        input_output_aliases={i: i for i in range(len(arrays))},
        name="tie",
    )(*arrays, *tokens)


class Flow:
    def __init__(self):
        self.active = {}
        self.results = {}
        self.deps = []

    def start(self, name, steps):
        self._request(name, steps, next(steps))

    def _request(self, name, steps, wanted):
        self.deps += [array for array, _, _ in wanted]
        self.active[name] = (steps, [swap(*want) for want in wanted])

    def meet(self, tokens, *names, more=()):
        names = [n for n in names if n in self.active]
        held = [array for n in names for array in self.active[n][1]]
        held = tie([*more, *held], tokens)
        more, held = held[: len(more)], held[len(more) :]
        self.deps += more
        for name in names:
            steps, arrays = self.active[name]
            arrays, held = held[: len(arrays)], held[len(arrays) :]
            self.deps += arrays
            try:
                self._request(name, steps, steps.send(arrays))
            except StopIteration as end:
                del self.active[name]
                self.results[name] = end.value
        return more

    def take(self):
        deps, self.deps = self.deps, []
        return deps


def part(vector, index):
    return vector[:, index * D : (index + 1) * D]


def forward_vectors(gains, vectors, layer):
    vector, below = vectors[layer], vectors[layer + 1]
    return (
        part(vector, 3),
        part(vector, 1),
        part(vector, 2),
        gains[layer + 1],
        part(below, 0),
    )


def gather(value):
    return lax.all_gather(value, "shard", axis=0, tiled=True)


def scattered(value):
    return lax.psum_scatter(value, "shard", scatter_dimension=0, tiled=True)


def ring_device(
    hidden,
    segments,
    pad_mask,
    encoder,
    src_len,
    grad_out,
    ln_gain,
    self_qkv,
    self_out,
    self_vec,
    cross_qkv,
    cross_out,
    cross_vec,
    fc_in,
    fc_out,
    mlp_vec,
):
    shards = lax.axis_size("shard")
    factor = 1.0 / math.sqrt(ROWS * lax.axis_size("rep") * shards)
    me = lax.axis_index("shard").astype(jnp.int32)
    scalars = jnp.stack([me, src_len[0]])
    flow = Flow()
    ff = fc_in.shape[1]

    gains, *vectors = gather_vectors(ln_gain, self_vec, cross_vec, mlp_vec)
    all_one = gather(jnp.concatenate([self_qkv, self_out], 1))
    all_two = gather(jnp.concatenate([cross_qkv, cross_out], 1))
    held_one, held_two = (WHOLE, [all_one]), (WHOLE, [all_two])
    all_in = gather(fc_in)
    rows = fc_out.shape[0] // 2
    low_out = gather(fc_out[:rows])
    flow.start("high", spread(fc_out[rows:], 0))
    encoded = encoder.reshape(ROWS, D)
    enc_t = encoded.T
    masks = (segments.reshape(ROWS, 1), segments.reshape(1, ROWS), pad_mask.reshape(1, ROWS))
    a_one, a_one_t, bias = prepare(hidden, gains[0], part(vectors[0], 0), masks)
    out_sum = jnp.sum(grad_out.astype(F32), 0)
    flow.take()
    flow.meet([a_one_t, enc_t], "high")
    x_one, a_two, a_two_t, *saved_one = attend_forward(
        scalars,
        hidden,
        a_one,
        bias,
        forward_vectors(gains, vectors, 0),
        held_one,
        deps=flow.take(),
    )
    flow.meet([a_two], "high")
    flow.meet([saved_one[4]], "high")
    layout, high_parts = flow.results["high"]
    layout = ((None, 0, rows),) + tuple((r, rows + first, count) for r, first, count in layout)
    held_out = (layout, [low_out, *high_parts])
    flow.take()
    x_two, a_three, a_three_t, *saved_two = attend_forward(
        scalars, x_one, a_two, encoded, forward_vectors(gains, vectors, 1), held_two
    )
    active, slope, grad_w2 = mlp_up(a_three, grad_out, all_in, part_from(vectors[2], 2))
    scattered_out = scattered(grad_w2)
    grad_w1, sum_fc, grad_two, gb_two, ga_two, gain_three, shift_three, out_two = mlp_down(
        scalars, a_three_t, grad_out, slope, all_in, x_two, gains[2], held_out, held_two
    )
    scattered_in = scattered(grad_w1)
    halves_two, *weights_two, q_two, v_two = attend_backward(
        scalars, 0, GROUPS, a_two_t, enc_t, ga_two, saved_two, gb_two, False
    )
    (scattered_out,) = flow.meet([v_two], more=[scattered_out])
    flow.start("out", over_copies(scattered_out))
    flow.start("cross", reduce(*weights_two))
    grad_one, gain_two, shift_two, grad_enc, out_one, gb_one, ga_one = project_back(
        scalars,
        [halves_two],
        grad_two,
        x_one,
        gains[1],
        held_two,
        held_one,
        deps=flow.take(),
    )
    flow.meet([gain_two], "cross", "out")
    early = [gain_three[0], shift_three[0], out_sum, sum_fc[0]]
    early += [gain_two[0], shift_two[0], q_two[0], v_two[0], out_two[0]]
    flow.start("early", sum_everywhere(jnp.concatenate(early)))
    grads_one, weights_one, q_one, v_one = attend_backward(
        scalars,
        0,
        GROUPS,
        a_one_t,
        bias,
        ga_one,
        saved_one,
        gb_one,
        True,
        deps=flow.take(),
    )
    (weights_one,) = flow.meet([v_one], "cross", "out", "early", more=[weights_one])
    scattered_one = scattered(weights_one)
    grad_hidden, gain_one, shift_one = project_back(
        scalars, [grads_one], grad_one, hidden, gains[0], held_one, deps=flow.take()
    )
    flow.meet([gain_one], "cross", "out", "early")
    late = [gain_one[0], shift_one[0], q_one[0], v_one[0], out_one[0]]
    flow.start("late", sum_everywhere(jnp.concatenate(late)))
    output = mlp_out(
        scalars, active, x_two, part(vectors[2], 1), held_out, deps=flow.take()
    )
    scattered_one, scattered_in = flow.meet(
        [output], "cross", "early", "late", more=[scattered_one, scattered_in]
    )
    summed_in = lax.psum(scattered_in, "rep")
    flow.start("self", over_copies(scattered_one[0]))
    while flow.active:
        flow.meet(flow.take(), *flow.active)
    done = flow.results

    def own(vector):
        size = vector.shape[0] // shards
        return lax.dynamic_slice_in_dim(vector, me * size, size) * factor

    base = 3 * D + ff
    early, late = done["early"], done["late"]
    grad_gain = jnp.stack([own(late[:D]), own(early[base : base + D]), own(early[:D])], 0)
    return (
        output,
        grad_hidden,
        grad_enc.reshape(1, ROWS, D),
        grad_gain,
        *join_heads([done["self"]], factor),
        own(late[D:]),
        *join_heads([done["cross"]], factor),
        own(early[base + D :]),
        summed_in.astype(F32) * factor,
        done["out"].astype(F32) * factor,
        own(early[D:base]),
    )


def part_from(vector, index):
    return vector[:, index * D :]


def gather_device(
    hidden,
    segments,
    pad_mask,
    encoder,
    src_len,
    grad_out,
    ln_gain,
    self_qkv,
    self_out,
    self_vec,
    cross_qkv,
    cross_out,
    cross_vec,
    fc_in,
    fc_out,
    mlp_vec,
):
    shards = lax.axis_size("shard")
    factor = 1.0 / math.sqrt(ROWS * lax.axis_size("rep") * shards)
    scalars = jnp.stack([jnp.int32(0), src_len[0]])
    encoded = encoder.reshape(ROWS, D)
    enc_t = encoded.T
    gains, *vectors = gather_vectors(ln_gain, self_vec, cross_vec, mlp_vec)
    held_one = (WHOLE, [gather(jnp.concatenate([self_qkv, self_out], 1))])
    held_two = (WHOLE, [gather(jnp.concatenate([cross_qkv, cross_out], 1))])
    all_in, held_out = gather(fc_in), (WHOLE_ROWS, [gather(fc_out)])
    masks = (segments.reshape(ROWS, 1), segments.reshape(1, ROWS), pad_mask.reshape(1, ROWS))
    a_one, a_one_t, bias = prepare(hidden, gains[0], part(vectors[0], 0), masks)
    x_one, a_two, a_two_t, *saved_one = attend_forward(
        scalars, hidden, a_one, bias, forward_vectors(gains, vectors, 0), held_one
    )
    x_two, a_three, a_three_t, *saved_two = attend_forward(
        scalars, x_one, a_two, encoded, forward_vectors(gains, vectors, 1), held_two
    )
    active, slope, grad_w2 = mlp_up(a_three, grad_out, all_in, part_from(vectors[2], 2))
    grad_w1, sum_fc, grad_two, gb_two, ga_two, gain_three, shift_three, out_two = mlp_down(
        scalars, a_three_t, grad_out, slope, all_in, x_two, gains[2], held_out, held_two
    )
    halves_two, weights_two, q_two, v_two = attend_backward(
        scalars, 0, GROUPS, a_two_t, enc_t, ga_two, saved_two, gb_two, True
    )
    grad_one, gain_two, shift_two, grad_enc, out_one, gb_one, ga_one = project_back(
        scalars, [halves_two], grad_two, x_one, gains[1], held_two, held_one
    )
    halves_one, weights_one, q_one, v_one = attend_backward(
        scalars, 0, GROUPS, a_one_t, bias, ga_one, saved_one, gb_one, True
    )
    grad_hidden, gain_one, shift_one = project_back(
        scalars, [halves_one], grad_one, hidden, gains[0], held_one
    )
    output = mlp_out(scalars, active, x_two, part(vectors[2], 1), held_out)

    def summed(value):
        return lax.psum(scattered(value.astype(BF16)), "rep")

    def final(value):
        return summed(value).astype(F32) * factor

    ones = [shift_one[0], q_one[0], v_one[0], out_one[0]]
    twos = [shift_two[0], q_two[0], v_two[0], out_two[0]]
    threes = [shift_three[0], jnp.sum(grad_out.astype(F32), 0), sum_fc[0]]
    gain = jnp.concatenate([gain_one, gain_two, gain_three], 0)
    return (
        output,
        grad_hidden,
        grad_enc.reshape(1, ROWS, D),
        final(gain.T).T,
        *join_heads([summed(weights_one.reshape(D, -1))], factor),
        final(jnp.concatenate(ones)),
        *join_heads([summed(weights_two.reshape(D, -1))], factor),
        final(jnp.concatenate(twos)),
        final(grad_w1),
        final(grad_w2),
        final(jnp.concatenate(threes)),
    )


def per_device(*arrays):
    copies = lax.axis_size("rep")
    if lax.axis_size("shard") == PIECES and copies & (copies - 1) == 0:
        return ring_device(*arrays)
    return gather_device(*arrays)


def solution(mesh):
    placed = (
        P(("rep", "shard"), None),
        P(("rep", "shard")),
        P(("rep", "shard")),
        P(("rep", "shard"), None, None),
        P(("rep", "shard")),
        P(("rep", "shard"), None),
        P(None, "shard"),
        P("shard", None),
        P("shard", None),
        P("shard"),
        P("shard", None),
        P("shard", None),
        P("shard"),
        P("shard", None),
        P("shard", None),
        P("shard"),
    )
    return jax.shard_map(
        per_device,
        mesh=mesh,
        in_specs=placed,
        out_specs=(
            P(("rep", "shard"), None),
            P(("rep", "shard"), None),
            P(("rep", "shard"), None, None),
            P(None, "shard"),
            P("shard", None),
            P("shard", None),
            P("shard"),
            P("shard", None),
            P("shard", None),
            P("shard"),
            P("shard", None),
            P("shard", None),
            P("shard"),
        ),
        check_vma=False,
    )
```
